256 devices in a mesh: mem: 32 (over x, z), cell: 8 (over y, core).
Axes of the slice: x: 4, y: 4, z: 8, core: 2. Of those that a mesh axis runs over, the one named last changes fastest.
Arguments:
- prior_states: bfloat16 [128, 4194304], P('mem', 'cell'), may hold values from -6 to 6
- measured_anomalies: bfloat16 [8, 256, 256, 128], P('cell', 'mem'), may hold values from -6 to 6
- departure_from_mean: bfloat16 [8, 256, 256], P('cell', 'mem'), may hold values from -6 to 6
- inverse_error_variance: bfloat16 [8, 256, 256], P('cell', 'mem'), may hold values from 0.25 to 4
- region_segment_indices: int32 [8, 256, 8], P('cell'), may hold values from 0 to 255, as said below
- active_slot_tallies: int32 [8, 256], P('cell'), may hold values from 4 to 8
- localization_coefficient: float32 [8, 256, 8], P('cell', 'mem'), may hold values from 0.2 to 1
Outputs:
- analysis: bfloat16 [128, 4194304], P('mem', 'cell')
The draws below stay inside these ranges and needn't reach their ends.
Inputs may be any that keep to these rules, and one draw needn't show every extreme that they name: `region_segment_indices`: entries index blocks of the patch's own cell block. Over the 8 patches i = m * 8 to m * 8 + 7 of one cell block taken together, the entries with one value of entry // 8 number at most 3, and exactly 3 for one such value.
All inputs are finite; a program needn't handle non-finite values.
Results may differ from the reference program's by a relative error of at most 0.006.
Values may be sent and summed in bfloat16 or wider, within the bound.
A program may use at most 128 MiB of HBM per device.

```python
import math
import jax
import jax.numpy as jnp
from jax import lax

ENSEMBLE_SIZE = 128
REGION_POINTS = 2048
PD = 8
NLIST = 8
OB = 256
BLK_DEV = 8
ITERS = 4
COLUMNS = 8
PATCH_COL = 256
BLK_COL = 256
DOMAIN_POINTS = 4194304
CAP = 3


def draw_region_segment_indices(key, part):
    key = jax.random.fold_in(key, 11)
    point_clusters = PATCH_COL // PD
    requests = PD * NLIST
    keys = jax.random.split(key, COLUMNS * point_clusters)

    def one_group(group_key):
        key_hot, key_slots, key_order, key_local = jax.random.split(group_key, 4)
        hottest = jax.random.randint(key_hot, (), 0, point_clusters)
        slots = jax.random.permutation(key_slots, (point_clusters - 1) * CAP)[:requests - CAP]
        others = (slots // CAP + hottest + 1) % point_clusters
        owners = jnp.concatenate([jnp.full((CAP,), hottest, jnp.int32), others.astype(jnp.int32)])
        owners = jax.random.permutation(key_order, owners)
        local = jax.random.randint(key_local, (requests,), 0, BLK_DEV)
        return (owners * BLK_DEV + local).astype(jnp.int32)
    chosen = jax.vmap(one_group)(keys)
    return chosen.reshape(COLUMNS, PATCH_COL, NLIST)


def place_ends(array, rng, low, high):
    dims = array.shape
    spot = [jax.random.randint(jax.random.fold_in(rng, axis), (), 0, dims[axis]) for axis in range(len(dims))]
    array = array.at[tuple(spot)].set(low)
    longest = dims.index(max(dims))
    spot[longest] = (spot[longest] + 1) % dims[longest]
    return array.at[tuple(spot)].set(high)


def shard_levels(key, extent, shards, least, top_value):
    level, own = 1.0, jax.random.fold_in(key, 6)
    for axis_at, blocks in shards:
        steps = jnp.exp(jax.random.uniform(jax.random.fold_in(own, axis_at), (blocks,), jnp.float32, least / len(shards), top_value / len(shards)))
        level = level * jnp.repeat(steps, extent[axis_at] // blocks).reshape([-1 if axis == axis_at else 1 for axis in range(len(extent))])
    return level


def centred(own_key, dims, scale, limit, pieces=(), kind=jnp.bfloat16):
    drawn = scale * jax.random.normal(own_key, dims, jnp.float32)
    if pieces:
        drawn = drawn * shard_levels(own_key, dims, pieces, -0.22, 0.18)
    return jnp.clip(drawn, -limit, limit).astype(kind)


def setup_inputs(seed: int = 0) -> dict:
    seeds = jax.random.split(jax.random.key(seed), 8)
    return {
        "prior_states": centred(seeds[0], (ENSEMBLE_SIZE, DOMAIN_POINTS), 1.0, 6.0, ((0, 32), (1, 8))),
        "measured_anomalies": centred(seeds[1], (COLUMNS, BLK_COL, OB, ENSEMBLE_SIZE), 1.0, 6.0, ((0, 8), (1, 32))),
        "departure_from_mean": centred(seeds[2], (COLUMNS, BLK_COL, OB), 1.0, 6.0, ((0, 8), (1, 32))),
        "inverse_error_variance": jnp.clip(jnp.exp(math.log(4.0) - 2.7725887 * jax.random.uniform(seeds[3], (COLUMNS, BLK_COL, OB), jnp.float32) ** shard_levels(seeds[3], (COLUMNS, BLK_COL, OB), ((0, 8), (1, 32)), -0.2, 0.2)), 0.25, 4.0).astype(jnp.bfloat16),
        "region_segment_indices": draw_region_segment_indices(jax.random.fold_in(seeds[7], 71), 0),
        "active_slot_tallies": place_ends(jax.random.randint(seeds[5], (COLUMNS, PATCH_COL), NLIST // 2, NLIST + 1), jax.random.fold_in(seeds[5], 1), NLIST // 2, NLIST).astype(jnp.int32),
        "localization_coefficient": jnp.clip(0.2 + 0.8 * jax.random.uniform(seeds[6], (COLUMNS, PATCH_COL, NLIST), jnp.float32) ** shard_levels(seeds[6], (COLUMNS, PATCH_COL, NLIST), ((0, 8), (1, 32)), -0.2, 0.2), 0.2, 1.0),
    }


HIGHEST = lax.Precision.HIGHEST

def select_patch(measured_anomalies, departure_from_mean, inverse_error_variance, region_segment_indices, active_slot_tallies, localization_coefficient, element_index):
    column = element_index // PATCH_COL
    within = element_index % PATCH_COL
    chosen = region_segment_indices[column, within]
    picked = measured_anomalies[column][chosen]
    values = departure_from_mean[column][chosen]
    scales = inverse_error_variance[column][chosen].astype(jnp.float32)
    active = (jnp.arange(NLIST) < active_slot_tallies[column, within]).astype(jnp.float32)
    weights = (localization_coefficient[column, within] * active)[:, None] * scales
    return (picked, values, weights)

def spread_terms(measured_anomalies, departure_from_mean, inverse_error_variance, region_segment_indices, active_slot_tallies, localization_coefficient, element_index):
    picked, values, weights = select_patch(measured_anomalies, departure_from_mean, inverse_error_variance, region_segment_indices, active_slot_tallies, localization_coefficient, element_index)
    power = jnp.sum(weights * jnp.square(values.astype(jnp.float32)))
    spread = jnp.sum(weights * lax.optimization_barrier(jnp.sum(jnp.square(picked.astype(jnp.float32)), axis=-1))) / (ENSEMBLE_SIZE - 1)
    return (power, spread)

def update_state_estimate(prior_states, measured_anomalies, departure_from_mean, inverse_error_variance, region_segment_indices, active_slot_tallies, localization_coefficient, variance_scaling_factor, element_index):
    picked, values, weights = select_patch(measured_anomalies, departure_from_mean, inverse_error_variance, region_segment_indices, active_slot_tallies, localization_coefficient, element_index)
    weighted = (picked.astype(jnp.float32) * weights[:, :, None]).astype(jnp.bfloat16).reshape(NLIST * OB, ENSEMBLE_SIZE)
    flat_obs = picked.reshape(NLIST * OB, ENSEMBLE_SIZE)
    gram_matrix = jnp.dot(weighted.T, flat_obs, preferred_element_type=jnp.float32)
    projected = jnp.dot(values.reshape(NLIST * OB), weighted, preferred_element_type=jnp.float32)
    identity = jnp.eye(ENSEMBLE_SIZE, dtype=jnp.float32)
    system = (ENSEMBLE_SIZE - 1) / variance_scaling_factor * identity + gram_matrix
    level = jnp.sqrt(jnp.sum(system * system))
    approach = system / level
    inverse_root = identity
    for sweep in range(ITERS):
        factor = 1.5 * identity - 0.5 * jnp.dot(inverse_root, approach, precision=HIGHEST)
        approach = jnp.dot(approach, factor, precision=HIGHEST)
        inverse_root = jnp.dot(factor, inverse_root, precision=HIGHEST)
    root = inverse_root / jnp.sqrt(level)
    mean_shift = jnp.dot(root, jnp.dot(root, projected, precision=HIGHEST), precision=HIGHEST)
    transform = (math.sqrt(ENSEMBLE_SIZE - 1) * root + mean_shift[:, None]).astype(jnp.bfloat16)
    realization_sequence = lax.dynamic_slice_in_dim(prior_states, element_index * REGION_POINTS, REGION_POINTS, 1)
    means = lax.optimization_barrier(jnp.mean(realization_sequence.astype(jnp.float32), axis=0))
    deviation = (realization_sequence.astype(jnp.float32) - means).astype(jnp.bfloat16)
    updated = means + jnp.dot(transform.T, deviation, preferred_element_type=jnp.float32)
    return updated.astype(jnp.bfloat16)

def reference(prior_states, measured_anomalies, departure_from_mean, inverse_error_variance, region_segment_indices, active_slot_tallies, localization_coefficient):
    element_indices = jnp.arange(COLUMNS * PATCH_COL, dtype=jnp.int32)
    power, spread = lax.map(lambda element_index: spread_terms(measured_anomalies, departure_from_mean, inverse_error_variance, region_segment_indices, active_slot_tallies, localization_coefficient, element_index), element_indices)
    variance_scaling_factor = jnp.sum(power) / jnp.sum(spread)
    region_sequence = lax.map(lambda element_index: update_state_estimate(prior_states, measured_anomalies, departure_from_mean, inverse_error_variance, region_segment_indices, active_slot_tallies, localization_coefficient, variance_scaling_factor, element_index), element_indices)
    return jnp.transpose(region_sequence, (1, 0, 2)).reshape(ENSEMBLE_SIZE, DOMAIN_POINTS)
```

```python
import functools
import math

import jax
import jax.numpy as jnp
from jax import lax
from jax.experimental import pallas as pl
from jax.experimental.pallas import tpu as pltpu
from jax.sharding import PartitionSpec as P

ITERS = 4
WINDOW = 2
CHUNK = 256
GROUP = 4

HIGHEST = lax.Precision.HIGHEST
MESH = pl.DeviceIdType.MESH
F32 = jnp.float32
BF16 = jnp.bfloat16


def iota(shape, axis):
    return lax.broadcasted_iota(jnp.int32, shape, axis)


def split(value):
    high = value.astype(BF16)
    return high, (value - high.astype(F32)).astype(BF16)


def fold(gram):
    half = gram.shape[0] // 2
    row, lane = iota((half, 2 * half), 0), iota((half, 2 * half), 1)
    return jnp.where(lane >= row, gram[:half], pltpu.roll(gram[half:], half, 1))


def unfold(folded, diagonal):
    half = folded.shape[0]
    row, lane = iota((2 * half, 2 * half), 0), iota((2 * half, 2 * half), 1)
    both = jnp.concatenate([folded, pltpu.roll(folded, half, 1)], axis=0)
    direct = ((row < half) & (lane >= row)) | ((row >= half) & (lane >= half) & (lane < row))
    full = jnp.where(direct, both, both.T)
    return jnp.where(row == lane, diagonal, full)


def product(left, right):
    return jnp.dot(left, right, precision=HIGHEST, preferred_element_type=F32)


def transforms(grams, projections, ridge):
    size = grams[0].shape[0]
    identity = (iota((size, size), 0) == iota((size, size), 1)).astype(F32)
    systems = [ridge * identity + gram for gram in grams]
    levels = [jnp.sqrt(jnp.sum(system * system, keepdims=True)) for system in systems]
    approach = [system / level for system, level in zip(systems, levels)]
    inverse_root = [None] * len(grams)
    for sweep in range(ITERS):
        if sweep == 0:
            factor = [1.5 * identity - 0.5 * a for a in approach]
        else:
            factor = [1.5 * identity - 0.5 * product(r, a) for r, a in zip(inverse_root, approach)]
        if sweep < ITERS - 1:
            approach = [product(a, f) for a, f in zip(approach, factor)]
        inverse_root = factor if sweep == 0 else [product(f, r) for f, r in zip(factor, inverse_root)]
    result = []
    for inverse, level, projected in zip(inverse_root, levels, projections):
        root = inverse / jnp.sqrt(level)
        wide = jnp.broadcast_to(projected, (8, size))
        mean_shift = product(product(wide, root), root)[:1]
        result.append((math.sqrt(size - 1) * root + mean_shift).astype(BF16))
    return result


def kernel(
    nx, nz, ncell,
    x_ref, y_ref, d_ref, e_ref, idx_ref, tally_ref, loc_ref,
    out_ref,
    arrived, result, grams, stats, partial, cells, flat, change, dep, prec,
    in_send, in_recv, in_self, small_send, small_recv, z_send, z_recv, x_send, x_recv,
    out_send, out_recv, out_self,
):
    n = nx * nz
    me, cell = lax.axis_index("mem"), lax.axis_index("cell")
    my_x, my_z = me // nz, me % nz
    patches, _, rows, points = arrived.shape
    blocks, obs, members = y_ref.shape
    half = members // 2
    nlist = loc_ref.shape[0] // patches

    def peer(dx, dz):
        return lax.rem(my_x + dx + nx, nx) * nz + lax.rem(my_z + dz + nz, nz)

    def offset(o):
        return lax.rem(me + o, n) if isinstance(o, int) and o == 0 else peer(o // nz, o % nz)

    def remote(src, dst, ssem, rsem, to):
        return pltpu.make_async_remote_copy(
            src_ref=src, dst_ref=dst, send_sem=ssem, recv_sem=rsem, device_id=to, device_id_type=MESH
        )

    def to_all(make):
        @pl.loop(1, n)
        def _(o):
            make(peer(o // nz, o % nz)).start()

    barrier = pltpu.get_barrier_semaphore()

    @pl.loop(1, n)
    def _(o):
        pl.semaphore_signal(barrier, inc=1, device_id={"mem": peer(o // nz, o % nz)}, device_id_type=MESH)

    @pl.loop(1, ncell)
    def _(o):
        pl.semaphore_signal(barrier, inc=1, device_id={"cell": lax.rem(cell + o, ncell)}, device_id_type=MESH)

    pl.semaphore_wait(barrier, n - 1 + ncell - 1)

    def columns(owner, p):
        return pl.ds(pl.multiple_of((owner * patches + p) * points, 128), points)

    def own_in(p):
        return pltpu.make_async_copy(x_ref.at[:, columns(me, p)], arrived.at[p, me], in_self.at[p])

    def wait_in_send(p):
        whole = arrived.at[p, pl.ds(0, n - 1)]
        remote(whole, whole, in_send.at[p], in_recv.at[p], {"mem": me}).wait_send()

    def issue(p):
        if p >= WINDOW:
            wait_in_send(p - WINDOW)
        own_in(p).start()
        to_all(
            lambda r: remote(x_ref.at[:, columns(r, p)], arrived.at[p, me], in_send.at[p], in_recv.at[p], {"mem": r})
        )

    issue(0)
    issue(1)

    dep[...] = d_ref[...].astype(F32)
    prec[...] = e_ref[...].astype(F32)
    lane = iota((1, members), 1)
    diagonal_mask = iota((members, members), 0) == iota((members, members), 1)

    @pl.loop(0, blocks)
    def _(b):
        y = y_ref[b]
        e, d = prec[pl.ds(b, 1), :], dep[pl.ds(b, 1), :]
        weighted = (y.astype(F32).T * e).astype(BF16)
        gram = jnp.dot(weighted, y, preferred_element_type=F32)
        high, low = split(e * d)
        row = iota((16, obs), 0)
        pair = jnp.where(row == 0, high.astype(F32), jnp.where(row == 1, low.astype(F32), 0.0)).astype(BF16)
        projected = jnp.sum(jnp.dot(pair, y, preferred_element_type=F32), axis=0, keepdims=True)
        diagonal = jnp.sum(jnp.where(diagonal_mask, gram, 0.0), axis=0, keepdims=True)
        tail = jnp.concatenate(
            [part.astype(F32) for part in split(diagonal) + split(projected)] + [jnp.zeros((4, members), F32)], axis=0
        )
        grams[me * blocks + b] = jnp.concatenate([fold(gram), tail], axis=0).astype(BF16)
        power = jnp.sum(e * d * d, keepdims=True)
        spread = jnp.sum(diagonal, keepdims=True)
        stats[me * blocks + b] = jnp.where(lane < half, power, spread)

    mine = pl.ds(me * blocks, blocks)

    def small_copy(which, buffer, place, to):
        return remote(buffer.at[place], buffer.at[place], small_send.at[which], small_recv.at[which], to)

    def wait_small(which, buffer, length):
        whole = buffer.at[pl.ds(0, length)]
        remote(whole, whole, small_send.at[which], small_recv.at[which], {"mem": me}).wait()

    to_all(lambda r: small_copy(0, stats, mine, {"mem": r}))

    first, second = (0, blocks // 2), (blocks // 2, blocks // 2)

    def along_z(piece, part, sem, step):
        start, size = part or (0, blocks)
        ref = grams.at[pl.ds(piece * blocks + start, size)]
        return remote(ref, ref, z_send.at[sem], z_recv.at[sem], {"mem": peer(0, step)})

    def along_x(piece):
        for dx in range(1, nx):
            ref = grams.at[pl.ds(piece * blocks, blocks)]
            remote(ref, ref, x_send.at[0], x_recv.at[0], {"mem": peer(dx, 0)}).start()

    reach = nz // 2

    def forward(step):
        last = step == reach - 1
        along_z(peer(0, -step), first if last else None, step, 1).start()
        along_z(peer(0, step), second if last else None, reach + step, -1).start()

    def receive(step):
        last = step == reach
        along_z(peer(0, -step), first if last else None, step - 1, 1).wait_recv()
        along_z(peer(0, step), second if last else None, reach + step - 1, -1).wait_recv()

    forward(0)
    along_x(me)
    issue(2)

    def weight(p, s):
        active = jnp.clip(tally_ref[p] - s, 0, 1).astype(F32)
        return loc_ref[p * nlist + s] * active

    wait_small(0, stats, (n - 1) * blocks)

    def add_request(i, total):
        p, s = i // nlist, i % nlist
        return total + weight(p, s) * stats[idx_ref[i]]

    share = lax.fori_loop(0, patches * nlist, add_request, jnp.zeros((1, members), F32))
    mine_partial = pl.ds(pl.multiple_of(me * 8, 8), 8)
    partial[mine_partial, :] = jnp.where(iota((8, members), 0) == 0, share, 0.0)
    to_all(lambda r: small_copy(1, partial, mine_partial, {"mem": r}))

    receive(1)
    forward(1)
    along_x(peer(0, -1))
    along_x(peer(0, 1))
    issue(3)

    wait_small(1, partial, (n - 1) * 8)
    mine_cell = pl.ds(pl.multiple_of(cell * 8, 8), 8)
    group_sum = jnp.sum(partial[...], axis=0, keepdims=True)
    cells[mine_cell, :] = jnp.where(iota((8, members), 0) == 0, group_sum, 0.0)

    @pl.loop(1, ncell)
    def _(o):
        small_copy(2, cells, mine_cell, {"cell": lax.rem(cell + o, ncell)}).start()

    receive(2)
    forward(2)
    along_x(peer(0, -2))
    along_x(peer(0, 2))
    issue(4)
    receive(3)
    forward(3)
    along_x(peer(0, -3))
    along_x(peer(0, 3))
    issue(5)
    receive(4)
    along_x(peer(0, 4))
    issue(6)

    wait_small(2, cells, (ncell - 1) * 8)
    sums = jnp.sum(cells[...], axis=0, keepdims=True)
    power = jnp.sum(jnp.where(lane == 0, sums, 0.0), keepdims=True)
    spread = jnp.sum(jnp.where(lane == half, sums, 0.0), keepdims=True) / (members - 1)
    ridge = (members - 1) / (power / spread)

    issue(7)
    from_x = grams.at[pl.ds(0, nz * (nx - 1) * blocks)]
    remote(from_x, from_x, x_send.at[0], x_recv.at[0], {"mem": me}).wait()
    for step in range(reach):
        last = step == reach - 1
        along_z(peer(0, -step), first if last else None, step, 1).wait_send()
        along_z(peer(0, step), second if last else None, reach + step, -1).wait_send()

    def collect(p):
        def add(s, total):
            return total + weight(p, s) * grams[idx_ref[p * nlist + s]].astype(F32)

        total = lax.fori_loop(0, nlist, add, jnp.zeros(grams.shape[1:], F32))
        gram, diagonal = total[:half], total[half : half + 1] + total[half + 1 : half + 2]
        projected = total[half + 2 : half + 3] + total[half + 3 : half + 4]
        return unfold(gram, diagonal), projected

    @pl.loop(0, patches // GROUP)
    def _(g):
        pairs = [collect(g * GROUP + k) for k in range(GROUP)]
        made = transforms([a for a, _ in pairs], [b for _, b in pairs], ridge)
        for k in range(GROUP):
            change[g * GROUP + k] = made[k]

    @pl.loop(0, patches)
    def _(p):
        whole = arrived.at[p, pl.ds(0, n - 1)]
        remote(whole, whole, in_send.at[p], in_recv.at[p], {"mem": me}).wait_recv()
        own_in(p).wait()

        @pl.loop(0, points // CHUNK)
        def _(c):
            cut = pl.ds(pl.multiple_of(c * CHUNK, CHUNK), CHUNK)
            for m in range(n):
                flat[rows * m : rows * (m + 1), :] = arrived[p, m, :, cut].astype(F32)
            states = flat[...]
            means = jnp.sum(states, axis=0, keepdims=True) * (1.0 / members)
            deviation = (states - means).astype(BF16)
            updated = means + jnp.dot(change[p], deviation, preferred_element_type=F32)
            for m in range(n):
                result[p, m, :, cut] = updated[rows * m : rows * (m + 1), :].astype(BF16)

        pltpu.make_async_copy(result.at[p, me], out_ref.at[:, columns(me, p)], out_self.at[0]).start()
        to_all(
            lambda r: remote(
                result.at[p, r], out_ref.at[:, columns(me, p)], out_send.at[0], out_recv.at[0], {"mem": r}
            )
        )

    for p in range(patches - WINDOW, patches):
        wait_in_send(p)
    mine_out = pl.ds(pl.multiple_of(me * patches * points, 128), patches * points)
    pltpu.make_async_copy(out_ref.at[:, mine_out], out_ref.at[:, mine_out], out_self.at[0]).wait()
    others = out_ref.at[:, pl.ds(0, (n - 1) * patches * points)]
    remote(others, others, out_send.at[0], out_recv.at[0], {"mem": me}).wait()


def body(nx, nz, ncell, prior_states, anomalies, departure, precision, lists, tallies, localization):
    n = nx * nz
    me = lax.axis_index("mem")
    rows, cells = prior_states.shape
    patches, nlist = localization.shape[1:]
    points = cells // (n * patches)
    blocks, obs, members = anomalies.shape[1:]
    own_lists = lax.dynamic_slice_in_dim(lists[0], me * patches, patches, 0).reshape(-1)
    own_counts = lax.dynamic_slice_in_dim(tallies[0], me * patches, patches, 0)
    vmem, smem, anywhere = (pl.BlockSpec(memory_space=s) for s in (pltpu.VMEM, pltpu.SMEM, pl.ANY))
    dma = pltpu.SemaphoreType.DMA
    return pl.pallas_call(
        functools.partial(kernel, nx, nz, ncell),
        out_shape=jax.ShapeDtypeStruct((rows, cells), BF16),
        in_specs=[anywhere, vmem, vmem, vmem, smem, smem, smem],
        out_specs=anywhere,
        scratch_shapes=[
            pltpu.VMEM((patches, n, rows, points), BF16),
            pltpu.VMEM((patches, n, rows, points), BF16),
            pltpu.VMEM((n * blocks, members // 2 + 8, members), BF16),
            pltpu.VMEM((n * blocks, 1, members), F32),
            pltpu.VMEM((n * 8, members), F32),
            pltpu.VMEM((ncell * 8, members), F32),
            pltpu.VMEM((members, CHUNK), F32),
            pltpu.VMEM((patches, members, members), BF16),
            pltpu.VMEM((blocks, obs), F32),
            pltpu.VMEM((blocks, obs), F32),
            dma((patches,)),
            dma((patches,)),
            dma((patches,)),
            dma((3,)),
            dma((3,)),
            dma((nz,)),
            dma((nz,)),
            dma((1,)),
            dma((1,)),
            dma((1,)),
            dma((1,)),
            dma((1,)),
        ],
        compiler_params=pltpu.CompilerParams(
            collective_id=0, has_side_effects=True, vmem_limit_bytes=56 * 2**20
        ),
        name="analysis_kernel",
    )(
        prior_states, anomalies[0], departure[0], precision[0], own_lists, own_counts, localization[0].reshape(-1)
    )


def solution(mesh):
    nx, nz = 4, mesh.shape["mem"] // 4
    return jax.shard_map(
        functools.partial(body, nx, nz, mesh.shape["cell"]),
        mesh=mesh,
        in_specs=(
            P("mem", "cell"),
            P("cell", "mem", None, None),
            P("cell", "mem", None),
            P("cell", "mem", None),
            P("cell", None, None),
            P("cell", None),
            P("cell", "mem", None),
        ),
        out_specs=P("mem", "cell"),
        check_vma=False,
    )
```

```python
import functools
import math

import jax
import jax.numpy as jnp
from jax import lax
from jax.experimental import pallas as pl
from jax.experimental.pallas import tpu as pltpu
from jax.sharding import PartitionSpec as P

ITERS = 4
WINDOW = 6
PACE = 4
BATCH = 8
CHUNK = 256
GROUP = 4

HIGHEST = lax.Precision.HIGHEST
MESH = pl.DeviceIdType.MESH
F32 = jnp.float32
BF16 = jnp.bfloat16


def iota(shape, axis):
    return lax.broadcasted_iota(jnp.int32, shape, axis)


def split(value):
    high = value.astype(BF16)
    return high, (value - high.astype(F32)).astype(BF16)


def fold(gram):
    half = gram.shape[0] // 2
    row, lane = iota((half, 2 * half), 0), iota((half, 2 * half), 1)
    return jnp.where(lane >= row, gram[:half], pltpu.roll(gram[half:], half, 1))


def unfold(folded, diagonal):
    half = folded.shape[0]
    row, lane = iota((2 * half, 2 * half), 0), iota((2 * half, 2 * half), 1)
    both = jnp.concatenate([folded, pltpu.roll(folded, half, 1)], axis=0)
    direct = ((row < half) & (lane >= row)) | ((row >= half) & (lane >= half) & (lane < row))
    full = jnp.where(direct, both, both.T)
    return jnp.where(row == lane, diagonal, full)


def with_tail(folded, diagonal, projected):
    parts = split(diagonal) + split(projected)
    rows = [part.astype(F32) for part in parts] + [jnp.zeros((4, folded.shape[1]), F32)]
    return jnp.concatenate([folded] + rows, axis=0).astype(BF16)


def from_tail(whole):
    half = whole.shape[0] - 8
    row = [whole[half + k : half + k + 1] for k in range(4)]
    return whole[:half], row[0] + row[1], row[2] + row[3]


def product(left, right):
    return jnp.dot(left, right, precision=HIGHEST, preferred_element_type=F32)


def transforms(grams, projections, ridge):
    size = grams[0].shape[0]
    identity = (iota((size, size), 0) == iota((size, size), 1)).astype(F32)
    systems = [ridge * identity + gram for gram in grams]
    levels = [jnp.sqrt(jnp.sum(system * system, keepdims=True)) for system in systems]
    approach = [system / level for system, level in zip(systems, levels)]
    inverse_root = [None] * len(grams)
    for sweep in range(ITERS):
        if sweep == 0:
            factor = [1.5 * identity - 0.5 * a for a in approach]
        else:
            factor = [1.5 * identity - 0.5 * product(r, a) for r, a in zip(inverse_root, approach)]
        if sweep < ITERS - 1:
            approach = [product(a, f) for a, f in zip(approach, factor)]
        inverse_root = factor if sweep == 0 else [product(f, r) for f, r in zip(factor, inverse_root)]
    result = []
    for inverse, level, projected in zip(inverse_root, levels, projections):
        root = inverse / jnp.sqrt(level)
        wide = jnp.broadcast_to(projected, (8, size))
        mean_shift = product(product(wide, root), root)[:1]
        result.append((math.sqrt(size - 1) * root + mean_shift).astype(BF16))
    return result


def kernel(
    nx, nz, ncell,
    x_ref, y_any, d_any, e_any, idx_any, tally_any, loc_any,
    out_ref,
    arrived, result, grams, sums_out, sums_in, sums_own, stats, partial, cells, flat, change, dep, prec,
    y_ref, d_ref, e_ref, locs, idx_ref, tally_ref, loc_ref,
    in_send, in_recv, in_self, small_send, small_recv, z_send, z_recv, x_send, x_recv,
    out_send, out_recv, out_self, load,
):
    n = nx * nz
    me, cell = lax.axis_index("mem"), lax.axis_index("cell")
    my_x, my_z = me // nz, me % nz
    patches, _, rows, points = arrived.shape
    blocks, obs, members = y_ref.shape
    half = members // 2
    nlist = loc_ref.shape[2]
    line = nz * blocks

    def peer(dx, dz):
        return lax.rem(my_x + dx + nx, nx) * nz + lax.rem(my_z + dz + nz, nz)

    def remote(src, dst, ssem, rsem, to):
        return pltpu.make_async_remote_copy(
            src_ref=src, dst_ref=dst, send_sem=ssem, recv_sem=rsem, device_id=to, device_id_type=MESH
        )

    def to_all(make):
        @pl.loop(1, n)
        def _(o):
            make(peer(o // nz, o % nz)).start()

    barrier = pltpu.get_barrier_semaphore()

    @pl.loop(1, n)
    def _(o):
        pl.semaphore_signal(barrier, inc=1, device_id={"mem": peer(o // nz, o % nz)}, device_id_type=MESH)

    @pl.loop(1, ncell)
    def _(o):
        pl.semaphore_signal(barrier, inc=1, device_id={"cell": lax.rem(cell + o, ncell)}, device_id_type=MESH)

    loads = [
        pltpu.make_async_copy(src, dst, load.at[k])
        for k, (src, dst) in enumerate(
            [(y_any, y_ref), (d_any, d_ref), (e_any, e_ref), (loc_any, locs.at[my_x]), (idx_any, idx_ref), (tally_any, tally_ref)]
        )
    ]
    for copy in loads:
        copy.start()

    pl.semaphore_wait(barrier, n - 1 + ncell - 1)

    def columns(owner, p):
        return pl.ds(pl.multiple_of((owner * patches + p) * points, 128), points)

    def own_in(p):
        return pltpu.make_async_copy(x_ref.at[:, columns(me, p)], arrived.at[p, me], in_self.at[p])

    batches = [(p, first) for p in range(patches) for first in range(1, n, BATCH)]
    sent, left = [], []

    def wait_in_send(k):
        p, first = batches[k]
        size = min(BATCH, n - first)
        ref = arrived.at[p, pl.ds(0, size)]
        remote(ref, ref, in_send.at[k], in_recv.at[p], {"mem": me}).wait_send()

    def pump(count=len(batches), window=WINDOW):
        for k in range(len(sent), min(len(sent) + count, len(batches))):
            p, first = batches[k]
            if k >= window:
                wait_in_send(k - window)
                left.append(k - window)
            if first == 1:
                own_in(p).start()

            @pl.loop(first, min(first + BATCH, n))
            def _(o):
                r = peer(o // nz, o % nz)
                remote(
                    x_ref.at[:, columns(r, p)], arrived.at[p, me], in_send.at[k], in_recv.at[p], {"mem": r}
                ).start()

            sent.append(k)

    pump(WINDOW)

    loads[3].wait()
    for dx in range(1, nx):
        ref = locs.at[my_x]
        remote(ref, ref, small_send.at[2], small_recv.at[2], {"mem": peer(dx, 0)}).start()
    for copy in loads[:3]:
        copy.wait()

    dep[...] = d_ref[...].astype(F32)
    prec[...] = e_ref[...].astype(F32)
    lane = iota((1, members), 1)
    diagonal_mask = iota((members, members), 0) == iota((members, members), 1)

    def one_block(b, tallied):
        y = y_ref[b]
        e, d = prec[pl.ds(b, 1), :], dep[pl.ds(b, 1), :]
        weighted = (y.astype(F32).T * e).astype(BF16)
        gram = jnp.dot(weighted, y, preferred_element_type=F32)
        high, low = split(e * d)
        row = iota((16, obs), 0)
        pair = jnp.where(row == 0, high.astype(F32), jnp.where(row == 1, low.astype(F32), 0.0)).astype(BF16)
        projected = jnp.sum(jnp.dot(pair, y, preferred_element_type=F32), axis=0, keepdims=True)
        diagonal = jnp.sum(jnp.where(diagonal_mask, gram, 0.0), axis=0, keepdims=True)
        grams[my_z * blocks + b] = with_tail(fold(gram), diagonal, projected)
        power = jnp.sum(e * d * d, keepdims=True)
        spread = jnp.sum(diagonal, keepdims=True)
        return tallied + jnp.where(lane == b, power, 0.0) + jnp.where(lane == blocks + b, spread, 0.0)

    stats[me] = lax.fori_loop(0, blocks, one_block, jnp.zeros((1, members), F32))

    def small_copy(which, buffer, place, to):
        return remote(buffer.at[place], buffer.at[place], small_send.at[which], small_recv.at[which], to)

    def wait_small(which, buffer):
        whole = buffer.at[pl.ds(0, buffer.shape[0] - 1)]
        remote(whole, whole, small_send.at[which], small_recv.at[which], {"mem": me}).wait()

    to_all(lambda r: small_copy(3, stats, me, {"mem": r}))

    first, second = (0, blocks // 2), (blocks // 2, blocks // 2)

    def along_z(shift, part, sem, step):
        start, size = part or (0, blocks)
        ref = grams.at[pl.ds(lax.rem(my_z + shift + nz, nz) * blocks + start, size)]
        return remote(ref, ref, z_send.at[sem], z_recv.at[sem], {"mem": peer(0, step)})

    reach = nz // 2

    def forward(step):
        last = step == reach - 1
        for block in range(blocks):
            if not last or block < blocks // 2:
                along_z(-step, (block, 1), step, 1).start()
            if not last or block >= blocks // 2:
                along_z(step, (block, 1), reach + step, -1).start()

    def receive(step):
        last = step == reach
        along_z(-step, first if last else None, step - 1, 1).wait_recv()
        along_z(step, second if last else None, reach + step - 1, -1).wait_recv()

    forward(0)
    loads[4].wait()
    loads[5].wait()
    wait_small(2, locs)
    to_scalar = pltpu.make_async_copy(locs, loc_ref, load.at[6])
    to_scalar.start()
    to_scalar.wait()

    def weight(x, p, s):
        active = jnp.clip(tally_ref[0, (x * nz + my_z) * patches + p] - s, 0, 1).astype(F32)
        return loc_ref[x, p, s] * active

    def listed(x, p, s):
        return idx_ref[s, (x * nz + my_z) * patches + p]

    pump(PACE)

    def add_request(p, total):
        for s in range(nlist):
            far = jnp.abs(block_at - listed(my_x, p, s))
            total = total + weight(my_x, p, s) * (1 - jnp.minimum(far, 1)).astype(F32)
        return total

    row, column = iota((n, members), 0), iota((n, members), 1)
    block_at = jnp.where(column < 2 * blocks, row * blocks + column % blocks, -1)
    asked = lax.fori_loop(0, patches, add_request, jnp.zeros((n, members), F32))
    wait_small(3, stats)
    shares = asked * jnp.sum(stats[...], axis=1)
    partial[me] = jnp.sum(shares, axis=0, keepdims=True)
    to_all(lambda r: small_copy(0, partial, me, {"mem": r}))
    receive(1)
    forward(1)
    pump(PACE)

    wait_small(0, partial)
    cells[cell] = jnp.sum(partial[...], axis=0)

    @pl.loop(1, ncell)
    def _(o):
        small_copy(1, cells, cell, {"cell": lax.rem(cell + o, ncell)}).start()

    for step in range(2, reach):
        receive(step)
        forward(step)
        pump(PACE)
    receive(reach)

    def add_blocks(dx):
        x = lax.rem(my_x + dx, nx)

        @pl.loop(0, patches)
        def _(p):
            total = jnp.zeros(grams.shape[1:], F32)
            for s in range(nlist):
                blk = listed(x, p, s)
                far = jnp.abs((blk >> (line.bit_length() - 1)) - my_x)
                w = weight(x, p, s) * (1 - jnp.minimum(far, 1)).astype(F32)
                total = total + w * grams[blk & (line - 1)].astype(F32)
            if dx:
                sums_out[dx - 1, p] = with_tail(*from_tail(total))
                remote(
                    sums_out.at[dx - 1, p], sums_in.at[dx - 1, p], x_send.at[0], x_recv.at[0], {"mem": peer(dx, 0)}
                ).start()
            else:
                sums_own[p] = total

    for dx in range(1, nx):
        add_blocks(dx)
    add_blocks(0)
    pump(PACE)
    remote(sums_in, sums_in, x_send.at[0], x_recv.at[0], {"mem": me}).wait()

    wait_small(1, cells)
    sums = jnp.sum(cells[...], axis=0)
    power = jnp.sum(jnp.where(lane < blocks, sums, 0.0), keepdims=True)
    spread = jnp.sum(jnp.where((lane >= blocks) & (lane < 2 * blocks), sums, 0.0), keepdims=True) / (members - 1)
    ridge = (members - 1) / (power / spread)

    for step in range(reach):
        last = step == reach - 1
        along_z(-step, first if last else None, step, 1).wait_send()
        along_z(step, second if last else None, reach + step, -1).wait_send()

    pump(window=len(batches))

    def collect(p):
        total = sums_own[p]
        for k in range(nx - 1):
            total = total + sums_in[k, p].astype(F32)
        gram, diagonal, projected = from_tail(total)
        return unfold(gram, diagonal), projected

    @pl.loop(0, patches // GROUP)
    def _(g):
        pairs = [collect(g * GROUP + k) for k in range(GROUP)]
        made = transforms([a for a, _ in pairs], [b for _, b in pairs], ridge)
        for k in range(GROUP):
            change[g * GROUP + k] = made[k]

    @pl.loop(0, patches)
    def _(p):
        whole = arrived.at[p, pl.ds(0, n - 1)]
        remote(whole, whole, in_send.at[p], in_recv.at[p], {"mem": me}).wait_recv()
        own_in(p).wait()

        @pl.loop(0, points // CHUNK)
        def _(c):
            cut = pl.ds(pl.multiple_of(c * CHUNK, CHUNK), CHUNK)
            for m in range(n):
                flat[rows * m : rows * (m + 1), :] = arrived[p, m, :, cut].astype(F32)
            states = flat[...]
            means = jnp.sum(states, axis=0, keepdims=True) * (1.0 / members)
            deviation = (states - means).astype(BF16)
            updated = means + jnp.dot(change[p], deviation, preferred_element_type=F32)
            for m in range(n):
                result[p, m, :, cut] = updated[rows * m : rows * (m + 1), :].astype(BF16)

        pltpu.make_async_copy(result.at[p, me], out_ref.at[:, columns(me, p)], out_self.at[0]).start()
        to_all(
            lambda r: remote(
                result.at[p, r], out_ref.at[:, columns(me, p)], out_send.at[0], out_recv.at[0], {"mem": r}
            )
        )

    for k in range(len(left), len(batches)):
        wait_in_send(k)
    mine_out = pl.ds(pl.multiple_of(me * patches * points, 128), patches * points)
    pltpu.make_async_copy(out_ref.at[:, mine_out], out_ref.at[:, mine_out], out_self.at[0]).wait()
    others = out_ref.at[:, pl.ds(0, (n - 1) * patches * points)]
    remote(others, others, out_send.at[0], out_recv.at[0], {"mem": me}).wait()


def body(nx, nz, ncell, prior_states, anomalies, departure, precision, lists, tallies, localization):
    n = nx * nz
    rows, cells = prior_states.shape
    patches, nlist = localization.shape[1:]
    points = cells // (n * patches)
    blocks, obs, members = anomalies.shape[1:]
    anywhere = pl.BlockSpec(memory_space=pl.ANY)
    dma = pltpu.SemaphoreType.DMA
    return pl.pallas_call(
        functools.partial(kernel, nx, nz, ncell),
        out_shape=pltpu.VMEM((rows, cells), BF16),
        in_specs=[anywhere] * 7,
        out_specs=anywhere,
        scratch_shapes=[
            pltpu.VMEM((patches, n, rows, points), BF16),
            pltpu.VMEM((patches, n, rows, points), BF16),
            pltpu.VMEM((n // nx * blocks, members // 2 + 8, members), BF16),
            pltpu.VMEM((nx - 1, patches, members // 2 + 8, members), BF16),
            pltpu.VMEM((nx - 1, patches, members // 2 + 8, members), BF16),
            pltpu.VMEM((patches, members // 2 + 8, members), F32),
            pltpu.VMEM((n, 1, members), F32),
            pltpu.VMEM((n, 1, members), F32),
            pltpu.VMEM((ncell, 1, members), F32),
            pltpu.VMEM((members, CHUNK), F32),
            pltpu.VMEM((patches, members, members), BF16),
            pltpu.VMEM((blocks, obs), F32),
            pltpu.VMEM((blocks, obs), F32),
            pltpu.VMEM((blocks, obs, members), BF16),
            pltpu.VMEM((blocks, obs), BF16),
            pltpu.VMEM((blocks, obs), BF16),
            pltpu.VMEM((nx, patches, nlist), F32),
            pltpu.SMEM((nlist, lists.shape[1]), jnp.int32),
            pltpu.SMEM((1, lists.shape[1]), jnp.int32),
            pltpu.SMEM((nx, patches, nlist), F32),
            dma((patches * (-(-(n - 1) // BATCH)),)),
            dma((patches,)),
            dma((patches,)),
            dma((4,)),
            dma((4,)),
            dma((nz,)),
            dma((nz,)),
            dma((1,)),
            dma((1,)),
            dma((1,)),
            dma((1,)),
            dma((1,)),
            dma((7,)),
        ],
        compiler_params=pltpu.CompilerParams(
            collective_id=0, has_side_effects=True, vmem_limit_bytes=20 * 2**20
        ),
        name="analysis_kernel",
    )(
        *(
            pltpu.with_memory_space_constraint(operand, pltpu.HBM)
            for operand in (
                prior_states, anomalies[0], departure[0], precision[0], lists[0].T, tallies, localization[0]
            )
        )
    )


def solution(mesh):
    nx, nz = 4, mesh.shape["mem"] // 4
    return jax.shard_map(
        functools.partial(body, nx, nz, mesh.shape["cell"]),
        mesh=mesh,
        in_specs=(
            P("mem", "cell"),
            P("cell", "mem", None, None),
            P("cell", "mem", None),
            P("cell", "mem", None),
            P("cell", None, None),
            P("cell", None),
            P("cell", "mem", None),
        ),
        out_specs=P("mem", "cell"),
        check_vma=False,
    )
```

```python
import functools
import math

import jax
import jax.numpy as jnp
from jax import lax
from jax.experimental import pallas as pl
from jax.experimental.pallas import tpu as pltpu
from jax.sharding import PartitionSpec as P

ITERS = 4
WINDOW = 6
PACE = 4
BATCH = 8
CHUNK = 256
GROUP = 4

HIGHEST = lax.Precision.HIGHEST
MESH = pl.DeviceIdType.MESH
F32 = jnp.float32
BF16 = jnp.bfloat16


def iota(shape, axis):
    return lax.broadcasted_iota(jnp.int32, shape, axis)


def split(value):
    high = value.astype(BF16)
    return high, (value - high.astype(F32)).astype(BF16)


def fold(gram):
    half = gram.shape[0] // 2
    row, lane = iota((half, 2 * half), 0), iota((half, 2 * half), 1)
    return jnp.where(lane >= row, gram[:half], pltpu.roll(gram[half:], half, 1))


def unfold(folded, diagonal):
    half = folded.shape[0]
    row, lane = iota((2 * half, 2 * half), 0), iota((2 * half, 2 * half), 1)
    both = jnp.concatenate([folded, pltpu.roll(folded, half, 1)], axis=0)
    direct = ((row < half) & (lane >= row)) | ((row >= half) & (lane >= half) & (lane < row))
    full = jnp.where(direct, both, both.T)
    return jnp.where(row == lane, diagonal, full)


def with_tail(folded, diagonal, projected):
    parts = split(diagonal) + split(projected)
    rows = [part.astype(F32) for part in parts] + [jnp.zeros((4, folded.shape[1]), F32)]
    return jnp.concatenate([folded] + rows, axis=0).astype(BF16)


def from_tail(whole):
    half = whole.shape[0] - 8
    row = [whole[half + k : half + k + 1] for k in range(4)]
    return whole[:half], row[0] + row[1], row[2] + row[3]


def product(left, right):
    return jnp.dot(left, right, precision=HIGHEST, preferred_element_type=F32)


def transforms(grams, projections, ridge):
    size = grams[0].shape[0]
    identity = (iota((size, size), 0) == iota((size, size), 1)).astype(F32)
    systems = [ridge * identity + gram for gram in grams]
    levels = [jnp.sqrt(jnp.sum(system * system, keepdims=True)) for system in systems]
    approach = [system / level for system, level in zip(systems, levels)]
    inverse_root = [None] * len(grams)
    for sweep in range(ITERS):
        if sweep == 0:
            factor = [1.5 * identity - 0.5 * a for a in approach]
        else:
            factor = [1.5 * identity - 0.5 * product(r, a) for r, a in zip(inverse_root, approach)]
        if sweep < ITERS - 1:
            approach = [product(a, f) for a, f in zip(approach, factor)]
        inverse_root = factor if sweep == 0 else [product(f, r) for f, r in zip(factor, inverse_root)]
    result = []
    for inverse, level, projected in zip(inverse_root, levels, projections):
        root = inverse / jnp.sqrt(level)
        wide = jnp.broadcast_to(projected, (8, size))
        mean_shift = product(product(wide, root), root)[:1]
        result.append((math.sqrt(size - 1) * root + mean_shift).astype(BF16))
    return result


def kernel(
    nx, nz, ncell,
    x_ref, y_any, d_any, e_any, idx_any, tally_any, loc_any,
    out_ref,
    arrived, result, grams, sums_out, sums_in, sums_own, stats, partial, cells, flat, change, dep, prec, lines, tails,
    y_ref, d_ref, e_ref, locs, idx_ref, tally_ref, loc_ref,
    in_send, in_recv, in_self, small_send, small_recv, z_send, z_recv, tail_send, tail_recv, x_send, x_recv,
    out_send, out_recv, out_self, load,
):
    n = nx * nz
    me, cell = lax.axis_index("mem"), lax.axis_index("cell")
    my_x, my_z = me // nz, me % nz
    patches, _, rows, points = arrived.shape
    blocks, obs, members = y_ref.shape
    half = members // 2
    nlist = loc_ref.shape[2]
    line = nz * blocks

    def peer(dx, dz):
        return lax.rem(my_x + dx + nx, nx) * nz + lax.rem(my_z + dz + nz, nz)

    def remote(src, dst, ssem, rsem, to):
        return pltpu.make_async_remote_copy(
            src_ref=src, dst_ref=dst, send_sem=ssem, recv_sem=rsem, device_id=to, device_id_type=MESH
        )

    def partner(o):
        turned = o + (cell % 2) * (n - 2 * o)
        return peer(turned // nz, turned % nz)

    def to_all(make):
        @pl.loop(1, n)
        def _(o):
            make(partner(o)).start()

    barrier = pltpu.get_barrier_semaphore()

    for o in range(1, n):
        pl.semaphore_signal(barrier, inc=1, device_id={"mem": lax.rem(me + o, n)}, device_id_type=MESH)
    for o in range(1, ncell):
        pl.semaphore_signal(barrier, inc=1, device_id={"cell": lax.rem(cell + o, ncell)}, device_id_type=MESH)

    loads = [
        pltpu.make_async_copy(src, dst, load.at[k])
        for k, (src, dst) in enumerate(
            [(y_any, y_ref), (d_any, d_ref), (e_any, e_ref), (loc_any, locs.at[my_x]), (idx_any, idx_ref), (tally_any, tally_ref)]
        )
    ]
    for copy in loads:
        copy.start()

    pl.semaphore_wait(barrier, n - 1 + ncell - 1)

    def columns(owner, p):
        return pl.ds(pl.multiple_of((owner * patches + p) * points, 128), points)

    def own_in(p):
        return pltpu.make_async_copy(x_ref.at[:, columns(me, p)], arrived.at[p, me], in_self.at[p])

    batches = [(p, first) for p in range(patches) for first in range(1, n, BATCH)]
    sent, left = [], []

    def wait_in_send(k):
        p, first = batches[k]
        size = min(BATCH, n - first)
        ref = arrived.at[p, pl.ds(0, size)]
        remote(ref, ref, in_send.at[k], in_recv.at[p], {"mem": me}).wait_send()

    def pump(count=len(batches), window=WINDOW):
        for k in range(len(sent), min(len(sent) + count, len(batches))):
            p, first = batches[k]
            if k >= window:
                wait_in_send(k - window)
                left.append(k - window)
            if first == 1:
                own_in(p).start()

            @pl.loop(first, min(first + BATCH, n))
            def _(o):
                r = partner(o)
                remote(
                    x_ref.at[:, columns(r, p)], arrived.at[p, me], in_send.at[k], in_recv.at[p], {"mem": r}
                ).start()

            sent.append(k)

    pump(WINDOW)

    loads[3].wait()
    for dx in range(1, nx):
        ref = locs.at[my_x]
        remote(ref, ref, small_send.at[2], small_recv.at[2], {"mem": peer(dx, 0)}).start()
    for copy in loads[:3]:
        copy.wait()

    dep[...] = d_ref[...].astype(F32)
    prec[...] = e_ref[...].astype(F32)
    lane = iota((1, members), 1)
    diagonal_mask = iota((members, members), 0) == iota((members, members), 1)

    def one_block(b, tallied):
        y = y_ref[b]
        e, d = prec[pl.ds(b, 1), :], dep[pl.ds(b, 1), :]
        weighted = (y.astype(F32).T * e).astype(BF16)
        gram = jnp.dot(weighted, y, preferred_element_type=F32)
        high, low = split(e * d)
        row = iota((16, obs), 0)
        pair = jnp.where(row == 0, high.astype(F32), jnp.where(row == 1, low.astype(F32), 0.0)).astype(BF16)
        projected = jnp.sum(jnp.dot(pair, y, preferred_element_type=F32), axis=0, keepdims=True)
        diagonal = jnp.sum(jnp.where(diagonal_mask, gram, 0.0), axis=0, keepdims=True)
        grams[my_z * blocks + b] = fold(gram).astype(BF16)
        lines[pl.ds(b, 1), :] = diagonal
        lines[pl.ds(blocks + b, 1), :] = projected
        power = jnp.sum(e * d * d, keepdims=True)
        spread = jnp.sum(diagonal, keepdims=True)
        return tallied + jnp.where(lane == b, power, 0.0) + jnp.where(lane == blocks + b, spread, 0.0)

    stats[me] = lax.fori_loop(0, blocks, one_block, jnp.zeros((1, members), F32))
    tails[my_z] = lines[...].astype(BF16)

    def small_copy(which, buffer, place, to):
        return remote(buffer.at[place], buffer.at[place], small_send.at[which], small_recv.at[which], to)

    def wait_small(which, buffer):
        whole = buffer.at[pl.ds(0, buffer.shape[0] - 1)]
        remote(whole, whole, small_send.at[which], small_recv.at[which], {"mem": me}).wait()

    to_all(lambda r: small_copy(3, stats, me, {"mem": r}))

    first, second = (0, blocks // 2), (blocks // 2, blocks // 2)

    def along_z(shift, part, sem, step):
        start, size = part or (0, blocks)
        ref = grams.at[pl.ds(lax.rem(my_z + shift + nz, nz) * blocks + start, size)]
        return remote(ref, ref, z_send.at[sem], z_recv.at[sem], {"mem": peer(0, step)})

    def tail_along_z(shift, sem, step):
        ref = tails.at[lax.rem(my_z + shift + nz, nz)]
        return remote(ref, ref, tail_send.at[sem], tail_recv.at[sem], {"mem": peer(0, step)})

    reach = nz // 2

    def forward(step):
        last = step == reach - 1
        tail_along_z(-step, step, 1).start()
        if not last:
            tail_along_z(step, reach + step, -1).start()
        for block in range(blocks):
            if not last or block < blocks // 2:
                along_z(-step, (block, 1), step, 1).start()
            if not last or block >= blocks // 2:
                along_z(step, (block, 1), reach + step, -1).start()

    def receive(step):
        last = step == reach
        tail_along_z(-step, step - 1, 1).wait_recv()
        if not last:
            tail_along_z(step, reach + step - 1, -1).wait_recv()
        along_z(-step, first if last else None, step - 1, 1).wait_recv()
        along_z(step, second if last else None, reach + step - 1, -1).wait_recv()

    forward(0)
    loads[4].wait()
    loads[5].wait()
    wait_small(2, locs)
    to_scalar = pltpu.make_async_copy(locs, loc_ref, load.at[6])
    to_scalar.start()
    to_scalar.wait()

    def weight(x, p, s):
        active = jnp.clip(tally_ref[0, (x * nz + my_z) * patches + p] - s, 0, 1).astype(F32)
        return loc_ref[x, p, s] * active

    def listed(x, p, s):
        return idx_ref[s, (x * nz + my_z) * patches + p]

    pump(PACE)

    def add_request(p, total):
        for s in range(nlist):
            far = jnp.abs(block_at - listed(my_x, p, s))
            total = total + weight(my_x, p, s) * (1 - jnp.minimum(far, 1)).astype(F32)
        return total

    row, column = iota((n, members), 0), iota((n, members), 1)
    block_at = jnp.where(column < 2 * blocks, row * blocks + column % blocks, -1)
    asked = lax.fori_loop(0, patches, add_request, jnp.zeros((n, members), F32))
    wait_small(3, stats)
    shares = asked * jnp.sum(stats[...], axis=1)
    partial[me] = jnp.sum(shares, axis=0, keepdims=True)
    to_all(lambda r: small_copy(0, partial, me, {"mem": r}))
    receive(1)
    forward(1)
    pump(PACE)

    wait_small(0, partial)
    cells[cell] = jnp.sum(partial[...], axis=0)

    @pl.loop(1, ncell)
    def _(o):
        small_copy(1, cells, cell, {"cell": lax.rem(cell + o, ncell)}).start()

    for step in range(2, reach):
        receive(step)
        forward(step)
        pump(PACE)
    receive(reach)

    in_page = iota(lines.shape, 0) % blocks

    def add_blocks(dx):
        x = lax.rem(my_x + dx, nx)

        @pl.loop(0, patches)
        def _(p):
            total, rest = jnp.zeros(grams.shape[1:], F32), jnp.zeros(lines.shape, F32)
            for s in range(nlist):
                blk = listed(x, p, s)
                far = jnp.abs((blk >> (line.bit_length() - 1)) - my_x)
                w = weight(x, p, s) * (1 - jnp.minimum(far, 1)).astype(F32)
                place = blk & (line - 1)
                total = total + w * grams[place].astype(F32)
                hot = 1 - jnp.minimum(jnp.abs(in_page - (place & (blocks - 1))), 1)
                rest = rest + (w * hot.astype(F32)) * tails[place >> (blocks.bit_length() - 1)].astype(F32)
            diagonal = jnp.sum(rest[:blocks], axis=0, keepdims=True)
            projected = jnp.sum(rest[blocks:], axis=0, keepdims=True)
            if dx:
                sums_out[dx - 1, p] = with_tail(total, diagonal, projected)
                remote(
                    sums_out.at[dx - 1, p], sums_in.at[dx - 1, p], x_send.at[0], x_recv.at[0], {"mem": peer(dx, 0)}
                ).start()
            else:
                sums_own[p] = jnp.concatenate([total, diagonal, jnp.zeros_like(diagonal), projected, jnp.zeros((5, members), F32)], axis=0)

    for dx in range(1, nx):
        add_blocks(dx)
    add_blocks(0)
    pump(PACE)
    remote(sums_in, sums_in, x_send.at[0], x_recv.at[0], {"mem": me}).wait()

    wait_small(1, cells)
    sums = jnp.sum(cells[...], axis=0)
    power = jnp.sum(jnp.where(lane < blocks, sums, 0.0), keepdims=True)
    spread = jnp.sum(jnp.where((lane >= blocks) & (lane < 2 * blocks), sums, 0.0), keepdims=True) / (members - 1)
    ridge = (members - 1) / (power / spread)

    for step in range(reach):
        last = step == reach - 1
        tail_along_z(-step, step, 1).wait_send()
        if not last:
            tail_along_z(step, reach + step, -1).wait_send()
        along_z(-step, first if last else None, step, 1).wait_send()
        along_z(step, second if last else None, reach + step, -1).wait_send()

    pump(window=len(batches))

    def collect(p):
        total = sums_own[p]
        for k in range(nx - 1):
            total = total + sums_in[k, p].astype(F32)
        gram, diagonal, projected = from_tail(total)
        return unfold(gram, diagonal), projected

    @pl.loop(0, patches // GROUP)
    def _(g):
        pairs = [collect(g * GROUP + k) for k in range(GROUP)]
        made = transforms([a for a, _ in pairs], [b for _, b in pairs], ridge)
        for k in range(GROUP):
            change[g * GROUP + k] = made[k]

    @pl.loop(0, patches)
    def _(p):
        whole = arrived.at[p, pl.ds(0, n - 1)]
        remote(whole, whole, in_send.at[p], in_recv.at[p], {"mem": me}).wait_recv()
        own_in(p).wait()

        @pl.loop(0, points // CHUNK)
        def _(c):
            cut = pl.ds(pl.multiple_of(c * CHUNK, CHUNK), CHUNK)
            for m in range(n):
                flat[rows * m : rows * (m + 1), :] = arrived[p, m, :, cut].astype(F32)
            states = flat[...]
            means = jnp.sum(states, axis=0, keepdims=True) * (1.0 / members)
            deviation = (states - means).astype(BF16)
            updated = means + jnp.dot(change[p], deviation, preferred_element_type=F32)
            for m in range(n):
                result[p, m, :, cut] = updated[rows * m : rows * (m + 1), :].astype(BF16)

        pltpu.make_async_copy(result.at[p, me], out_ref.at[:, columns(me, p)], out_self.at[0]).start()
        to_all(
            lambda r: remote(
                result.at[p, r], out_ref.at[:, columns(me, p)], out_send.at[0], out_recv.at[0], {"mem": r}
            )
        )

    for k in range(len(left), len(batches)):
        wait_in_send(k)
    mine_out = pl.ds(pl.multiple_of(me * patches * points, 128), patches * points)
    pltpu.make_async_copy(out_ref.at[:, mine_out], out_ref.at[:, mine_out], out_self.at[0]).wait()
    others = out_ref.at[:, pl.ds(0, (n - 1) * patches * points)]
    remote(others, others, out_send.at[0], out_recv.at[0], {"mem": me}).wait()


def body(nx, nz, ncell, prior_states, anomalies, departure, precision, lists, tallies, localization):
    n = nx * nz
    rows, cells = prior_states.shape
    patches, nlist = localization.shape[1:]
    points = cells // (n * patches)
    blocks, obs, members = anomalies.shape[1:]
    anywhere = pl.BlockSpec(memory_space=pl.ANY)
    dma = pltpu.SemaphoreType.DMA
    return pl.pallas_call(
        functools.partial(kernel, nx, nz, ncell),
        out_shape=pltpu.VMEM((rows, cells), BF16),
        in_specs=[anywhere] * 7,
        out_specs=anywhere,
        scratch_shapes=[
            pltpu.VMEM((patches, n, rows, points), BF16),
            pltpu.VMEM((patches, n, rows, points), BF16),
            pltpu.VMEM((n // nx * blocks, members // 2, members), BF16),
            pltpu.VMEM((nx - 1, patches, members // 2 + 8, members), BF16),
            pltpu.VMEM((nx - 1, patches, members // 2 + 8, members), BF16),
            pltpu.VMEM((patches, members // 2 + 8, members), F32),
            pltpu.VMEM((n, 1, members), F32),
            pltpu.VMEM((n, 1, members), F32),
            pltpu.VMEM((ncell, 1, members), F32),
            pltpu.VMEM((members, CHUNK), F32),
            pltpu.VMEM((patches, members, members), BF16),
            pltpu.VMEM((blocks, obs), F32),
            pltpu.VMEM((blocks, obs), F32),
            pltpu.VMEM((2 * blocks, members), F32),
            pltpu.VMEM((n // nx, 2 * blocks, members), BF16),
            pltpu.VMEM((blocks, obs, members), BF16),
            pltpu.VMEM((blocks, obs), BF16),
            pltpu.VMEM((blocks, obs), BF16),
            pltpu.VMEM((nx, patches, nlist), F32),
            pltpu.SMEM((nlist, lists.shape[1]), jnp.int32),
            pltpu.SMEM((1, lists.shape[1]), jnp.int32),
            pltpu.SMEM((nx, patches, nlist), F32),
            dma((patches * (-(-(n - 1) // BATCH)),)),
            dma((patches,)),
            dma((patches,)),
            dma((4,)),
            dma((4,)),
            dma((nz,)),
            dma((nz,)),
            dma((nz,)),
            dma((nz,)),
            dma((1,)),
            dma((1,)),
            dma((1,)),
            dma((1,)),
            dma((1,)),
            dma((7,)),
        ],
        compiler_params=pltpu.CompilerParams(
            collective_id=0, has_side_effects=True, vmem_limit_bytes=20 * 2**20
        ),
        name="analysis_kernel",
    )(
        *(
            pltpu.with_memory_space_constraint(operand, pltpu.HBM)
            for operand in (
                prior_states, anomalies[0], departure[0], precision[0], lists[0].T, tallies, localization[0]
            )
        )
    )


def solution(mesh):
    nx, nz = 4, mesh.shape["mem"] // 4
    return jax.shard_map(
        functools.partial(body, nx, nz, mesh.shape["cell"]),
        mesh=mesh,
        in_specs=(
            P("mem", "cell"),
            P("cell", "mem", None, None),
            P("cell", "mem", None),
            P("cell", "mem", None),
            P("cell", None, None),
            P("cell", None),
            P("cell", "mem", None),
        ),
        out_specs=P("mem", "cell"),
        check_vma=False,
    )
```

```python
import functools
import math

import jax
import jax.numpy as jnp
from jax import lax
from jax.experimental import pallas as pl
from jax.experimental.pallas import tpu as pltpu
from jax.sharding import PartitionSpec as P

ITERS = 4
WINDOW = 6
PACE = 4
BATCH = 8
CHUNK = 256
GROUP = 4

HIGHEST = lax.Precision.HIGHEST
MESH = pl.DeviceIdType.MESH
F32 = jnp.float32
BF16 = jnp.bfloat16


def iota(shape, axis):
    return lax.broadcasted_iota(jnp.int32, shape, axis)


def split(value):
    high = value.astype(BF16)
    return high, (value - high.astype(F32)).astype(BF16)


def fold(gram):
    half = gram.shape[0] // 2
    row, lane = iota((half, 2 * half), 0), iota((half, 2 * half), 1)
    return jnp.where(lane >= row, gram[:half], pltpu.roll(gram[half:], half, 1))


def unfold(folded, diagonal):
    half = folded.shape[0]
    row, lane = iota((2 * half, 2 * half), 0), iota((2 * half, 2 * half), 1)
    both = jnp.concatenate([folded, pltpu.roll(folded, half, 1)], axis=0)
    direct = ((row < half) & (lane >= row)) | ((row >= half) & (lane >= half) & (lane < row))
    full = jnp.where(direct, both, both.T)
    return jnp.where(row == lane, diagonal, full)


def with_tail(folded, diagonal, projected):
    parts = split(diagonal) + split(projected)
    rows = [part.astype(F32) for part in parts] + [jnp.zeros((4, folded.shape[1]), F32)]
    return jnp.concatenate([folded] + rows, axis=0).astype(BF16)


def from_tail(whole):
    half = whole.shape[0] - 8
    row = [whole[half + k : half + k + 1] for k in range(4)]
    return whole[:half], row[0] + row[1], row[2] + row[3]


def product(left, right):
    return jnp.dot(left, right, precision=HIGHEST, preferred_element_type=F32)


def transforms(grams, projections, ridge):
    size = grams[0].shape[0]
    identity = (iota((size, size), 0) == iota((size, size), 1)).astype(F32)
    systems = [ridge * identity + gram for gram in grams]
    levels = [jnp.sqrt(jnp.sum(system * system, keepdims=True)) for system in systems]
    approach = [system / level for system, level in zip(systems, levels)]
    inverse_root = [None] * len(grams)
    for sweep in range(ITERS):
        if sweep == 0:
            factor = [1.5 * identity - 0.5 * a for a in approach]
        else:
            factor = [1.5 * identity - 0.5 * product(r, a) for r, a in zip(inverse_root, approach)]
        if sweep < ITERS - 1:
            approach = [product(a, f) for a, f in zip(approach, factor)]
        inverse_root = factor if sweep == 0 else [product(f, r) for f, r in zip(factor, inverse_root)]
    result = []
    for inverse, level, projected in zip(inverse_root, levels, projections):
        root = inverse / jnp.sqrt(level)
        wide = jnp.broadcast_to(projected, (8, size))
        mean_shift = product(product(wide, root), root)[:1]
        result.append((math.sqrt(size - 1) * root + mean_shift).astype(BF16))
    return result


def kernel(
    nx, nz, ncell,
    x_ref, y_any, d_any, e_any, idx_any, tally_any, loc_any,
    out_ref,
    arrived, result, grams, sums_out, sums_in, sums_own, stats, partial, cells, flat, change, dep, prec, lines, tails,
    y_ref, d_ref, e_ref, locs, idx_ref, tally_ref, loc_ref,
    in_send, in_recv, in_self, small_send, small_recv, z_send, z_recv, tail_send, tail_recv, x_send, x_recv,
    out_send, out_recv, out_self, load,
):
    n = nx * nz
    me, cell = lax.axis_index("mem"), lax.axis_index("cell")
    my_x, my_z = me // nz, me % nz
    patches, _, rows, points = arrived.shape
    blocks, obs, members = y_ref.shape
    half = members // 2
    nlist = loc_ref.shape[2]
    line = nz * blocks

    def peer(dx, dz):
        return lax.rem(my_x + dx + nx, nx) * nz + lax.rem(my_z + dz + nz, nz)

    def remote(src, dst, ssem, rsem, to):
        return pltpu.make_async_remote_copy(
            src_ref=src, dst_ref=dst, send_sem=ssem, recv_sem=rsem, device_id=to, device_id_type=MESH
        )

    def partner(o):
        turned = o + (cell % 2) * (n - 2 * o)
        return peer(turned // nz, turned % nz)

    def to_all(make):
        @pl.loop(1, n)
        def _(o):
            make(partner(o)).start()

    barrier = pltpu.get_barrier_semaphore()

    for o in range(1, n):
        pl.semaphore_signal(barrier, inc=1, device_id={"mem": lax.rem(me + o, n)}, device_id_type=MESH)
    for o in range(1, ncell):
        pl.semaphore_signal(barrier, inc=1, device_id={"cell": lax.rem(cell + o, ncell)}, device_id_type=MESH)

    loads = [
        pltpu.make_async_copy(src, dst, load.at[k])
        for k, (src, dst) in enumerate(
            [(y_any, y_ref), (d_any, d_ref), (e_any, e_ref), (loc_any, locs.at[my_x]), (idx_any, idx_ref), (tally_any, tally_ref)]
        )
    ]
    for copy in loads:
        copy.start()

    pl.semaphore_wait(barrier, n - 1 + ncell - 1)

    def columns(owner, p):
        return pl.ds(pl.multiple_of((owner * patches + p) * points, 128), points)

    def own_in(p):
        return pltpu.make_async_copy(x_ref.at[:, columns(me, p)], arrived.at[p, me], in_self.at[p])

    batches = [(p, first) for p in range(patches) for first in range(1, n, BATCH)]
    sent, left = [], []

    def wait_in_send(k):
        p, first = batches[k]
        size = min(BATCH, n - first)
        ref = arrived.at[p, pl.ds(0, size)]
        remote(ref, ref, in_send.at[k], in_recv.at[p], {"mem": me}).wait_send()

    def pump(count=len(batches), window=WINDOW):
        for k in range(len(sent), min(len(sent) + count, len(batches))):
            p, first = batches[k]
            if k >= window:
                wait_in_send(k - window)
                left.append(k - window)
            if first == 1:
                own_in(p).start()

            @pl.loop(first, min(first + BATCH, n))
            def _(o):
                r = partner(o)
                remote(
                    x_ref.at[:, columns(r, p)], arrived.at[p, me], in_send.at[k], in_recv.at[p], {"mem": r}
                ).start()

            sent.append(k)

    pump(WINDOW)

    loads[3].wait()
    for dx in range(1, nx):
        ref = locs.at[my_x]
        remote(ref, ref, small_send.at[2], small_recv.at[2], {"mem": peer(dx, 0)}).start()
    for copy in loads[:3]:
        copy.wait()

    dep[...] = d_ref[...].astype(F32)
    prec[...] = e_ref[...].astype(F32)
    lane = iota((1, members), 1)
    diagonal_mask = iota((members, members), 0) == iota((members, members), 1)

    def one_block(b, tallied):
        y = y_ref[b]
        e, d = prec[pl.ds(b, 1), :], dep[pl.ds(b, 1), :]
        weighted = (y.astype(F32).T * e).astype(BF16)
        gram = jnp.dot(weighted, y, preferred_element_type=F32)
        high, low = split(e * d)
        row = iota((16, obs), 0)
        pair = jnp.where(row == 0, high.astype(F32), jnp.where(row == 1, low.astype(F32), 0.0)).astype(BF16)
        projected = jnp.sum(jnp.dot(pair, y, preferred_element_type=F32), axis=0, keepdims=True)
        diagonal = jnp.sum(jnp.where(diagonal_mask, gram, 0.0), axis=0, keepdims=True)
        grams[my_z * blocks + b] = fold(gram).astype(BF16)
        lines[pl.ds(b, 1), :] = diagonal
        lines[pl.ds(blocks + b, 1), :] = projected
        power = jnp.sum(e * d * d, keepdims=True)
        spread = jnp.sum(diagonal, keepdims=True)
        return tallied + jnp.where(lane == b, power, 0.0) + jnp.where(lane == blocks + b, spread, 0.0)

    stats[me] = lax.fori_loop(0, blocks, one_block, jnp.zeros((1, members), F32))
    pairs = split(lines[:blocks, :]) + split(lines[blocks:, :])
    tails[my_z] = jnp.concatenate([part.astype(F32) for part in pairs], axis=0).astype(BF16)

    def small_copy(which, buffer, place, to):
        return remote(buffer.at[place], buffer.at[place], small_send.at[which], small_recv.at[which], to)

    def wait_small(which, buffer):
        whole = buffer.at[pl.ds(0, buffer.shape[0] - 1)]
        remote(whole, whole, small_send.at[which], small_recv.at[which], {"mem": me}).wait()

    to_all(lambda r: small_copy(3, stats, me, {"mem": r}))

    first, second = (0, blocks // 2), (blocks // 2, blocks // 2)

    def along_z(shift, part, sem, step):
        start, size = part or (0, blocks)
        ref = grams.at[pl.ds(lax.rem(my_z + shift + nz, nz) * blocks + start, size)]
        return remote(ref, ref, z_send.at[sem], z_recv.at[sem], {"mem": peer(0, step)})

    def tail_along_z(shift, sem, step):
        ref = tails.at[lax.rem(my_z + shift + nz, nz)]
        return remote(ref, ref, tail_send.at[sem], tail_recv.at[sem], {"mem": peer(0, step)})

    reach = nz // 2

    def forward(step):
        last = step == reach - 1
        tail_along_z(-step, step, 1).start()
        if not last:
            tail_along_z(step, reach + step, -1).start()
        for block in range(blocks):
            if not last or block < blocks // 2:
                along_z(-step, (block, 1), step, 1).start()
            if not last or block >= blocks // 2:
                along_z(step, (block, 1), reach + step, -1).start()

    def receive(step):
        last = step == reach
        tail_along_z(-step, step - 1, 1).wait_recv()
        if not last:
            tail_along_z(step, reach + step - 1, -1).wait_recv()
        along_z(-step, first if last else None, step - 1, 1).wait_recv()
        along_z(step, second if last else None, reach + step - 1, -1).wait_recv()

    forward(0)
    loads[4].wait()
    loads[5].wait()
    wait_small(2, locs)
    to_scalar = pltpu.make_async_copy(locs, loc_ref, load.at[6])
    to_scalar.start()
    to_scalar.wait()

    def weight(x, p, s):
        active = jnp.clip(tally_ref[0, (x * nz + my_z) * patches + p] - s, 0, 1).astype(F32)
        return loc_ref[x, p, s] * active

    def listed(x, p, s):
        return idx_ref[s, (x * nz + my_z) * patches + p]

    pump(PACE)

    def add_request(p, total):
        for s in range(nlist):
            far = jnp.abs(block_at - listed(my_x, p, s))
            total = total + weight(my_x, p, s) * (1 - jnp.minimum(far, 1)).astype(F32)
        return total

    row, column = iota((n, members), 0), iota((n, members), 1)
    block_at = jnp.where(column < 2 * blocks, row * blocks + column % blocks, -1)
    asked = lax.fori_loop(0, patches, add_request, jnp.zeros((n, members), F32))
    wait_small(3, stats)
    shares = asked * jnp.sum(stats[...], axis=1)
    partial[me] = jnp.sum(shares, axis=0, keepdims=True)
    to_all(lambda r: small_copy(0, partial, me, {"mem": r}))
    receive(1)
    forward(1)
    pump(PACE)

    wait_small(0, partial)
    cells[cell] = jnp.sum(partial[...], axis=0)

    @pl.loop(1, ncell)
    def _(o):
        small_copy(1, cells, cell, {"cell": lax.rem(cell + o, ncell)}).start()

    for step in range(2, reach):
        receive(step)
        forward(step)
        pump(PACE)
    receive(reach)

    in_page = iota(tails.shape[1:], 0) % blocks

    def add_blocks(dx):
        x = lax.rem(my_x + dx, nx)

        @pl.loop(0, patches)
        def _(p):
            total, rest = jnp.zeros(grams.shape[1:], F32), jnp.zeros(tails.shape[1:], F32)
            for s in range(nlist):
                blk = listed(x, p, s)
                far = jnp.abs((blk >> (line.bit_length() - 1)) - my_x)
                w = weight(x, p, s) * (1 - jnp.minimum(far, 1)).astype(F32)
                place = blk & (line - 1)
                total = total + w * grams[place].astype(F32)
                hot = 1 - jnp.minimum(jnp.abs(in_page - (place & (blocks - 1))), 1)
                rest = rest + (w * hot.astype(F32)) * tails[place >> (blocks.bit_length() - 1)].astype(F32)
            diagonal = jnp.sum(rest[: 2 * blocks], axis=0, keepdims=True)
            projected = jnp.sum(rest[2 * blocks :], axis=0, keepdims=True)
            if dx:
                sums_out[dx - 1, p] = with_tail(total, diagonal, projected)
                remote(
                    sums_out.at[dx - 1, p], sums_in.at[dx - 1, p], x_send.at[0], x_recv.at[0], {"mem": peer(dx, 0)}
                ).start()
            else:
                none = jnp.zeros_like(diagonal)
                sums_own[p] = jnp.concatenate([total, diagonal, none, projected] + [none] * 5, axis=0)

    for dx in range(1, nx):
        add_blocks(dx)
    add_blocks(0)
    pump(PACE)
    remote(sums_in, sums_in, x_send.at[0], x_recv.at[0], {"mem": me}).wait()

    wait_small(1, cells)
    sums = jnp.sum(cells[...], axis=0)
    power = jnp.sum(jnp.where(lane < blocks, sums, 0.0), keepdims=True)
    spread = jnp.sum(jnp.where((lane >= blocks) & (lane < 2 * blocks), sums, 0.0), keepdims=True) / (members - 1)
    ridge = (members - 1) / (power / spread)

    for step in range(reach):
        last = step == reach - 1
        tail_along_z(-step, step, 1).wait_send()
        if not last:
            tail_along_z(step, reach + step, -1).wait_send()
        along_z(-step, first if last else None, step, 1).wait_send()
        along_z(step, second if last else None, reach + step, -1).wait_send()

    pump(window=len(batches))

    def collect(p):
        total = sums_own[p]
        for k in range(nx - 1):
            total = total + sums_in[k, p].astype(F32)
        gram, diagonal, projected = from_tail(total)
        return unfold(gram, diagonal), projected

    @pl.loop(0, patches // GROUP)
    def _(g):
        pairs = [collect(g * GROUP + k) for k in range(GROUP)]
        made = transforms([a for a, _ in pairs], [b for _, b in pairs], ridge)
        for k in range(GROUP):
            change[g * GROUP + k] = made[k]

    @pl.loop(0, patches)
    def _(p):
        whole = arrived.at[p, pl.ds(0, n - 1)]
        remote(whole, whole, in_send.at[p], in_recv.at[p], {"mem": me}).wait_recv()
        own_in(p).wait()

        @pl.loop(0, points // CHUNK)
        def _(c):
            cut = pl.ds(pl.multiple_of(c * CHUNK, CHUNK), CHUNK)
            for m in range(n):
                flat[rows * m : rows * (m + 1), :] = arrived[p, m, :, cut].astype(F32)
            states = flat[...]
            means = jnp.sum(states, axis=0, keepdims=True) * (1.0 / members)
            deviation = (states - means).astype(BF16)
            updated = means + jnp.dot(change[p], deviation, preferred_element_type=F32)
            for m in range(n):
                result[p, m, :, cut] = updated[rows * m : rows * (m + 1), :].astype(BF16)

        pltpu.make_async_copy(result.at[p, me], out_ref.at[:, columns(me, p)], out_self.at[0]).start()
        to_all(
            lambda r: remote(
                result.at[p, r], out_ref.at[:, columns(me, p)], out_send.at[0], out_recv.at[0], {"mem": r}
            )
        )

    for k in range(len(left), len(batches)):
        wait_in_send(k)
    mine_out = pl.ds(pl.multiple_of(me * patches * points, 128), patches * points)
    pltpu.make_async_copy(out_ref.at[:, mine_out], out_ref.at[:, mine_out], out_self.at[0]).wait()
    others = out_ref.at[:, pl.ds(0, (n - 1) * patches * points)]
    remote(others, others, out_send.at[0], out_recv.at[0], {"mem": me}).wait()


def body(nx, nz, ncell, prior_states, anomalies, departure, precision, lists, tallies, localization):
    n = nx * nz
    rows, cells = prior_states.shape
    patches, nlist = localization.shape[1:]
    points = cells // (n * patches)
    blocks, obs, members = anomalies.shape[1:]
    anywhere = pl.BlockSpec(memory_space=pl.ANY)
    dma = pltpu.SemaphoreType.DMA
    return pl.pallas_call(
        functools.partial(kernel, nx, nz, ncell),
        out_shape=pltpu.VMEM((rows, cells), BF16),
        in_specs=[anywhere] * 7,
        out_specs=anywhere,
        scratch_shapes=[
            pltpu.VMEM((patches, n, rows, points), BF16),
            pltpu.VMEM((patches, n, rows, points), BF16),
            pltpu.VMEM((n // nx * blocks, members // 2, members), BF16),
            pltpu.VMEM((nx - 1, patches, members // 2 + 8, members), BF16),
            pltpu.VMEM((nx - 1, patches, members // 2 + 8, members), BF16),
            pltpu.VMEM((patches, members // 2 + 8, members), F32),
            pltpu.VMEM((n, 1, members), F32),
            pltpu.VMEM((n, 1, members), F32),
            pltpu.VMEM((ncell, 1, members), F32),
            pltpu.VMEM((members, CHUNK), F32),
            pltpu.VMEM((patches, members, members), BF16),
            pltpu.VMEM((blocks, obs), F32),
            pltpu.VMEM((blocks, obs), F32),
            pltpu.VMEM((2 * blocks, members), F32),
            pltpu.VMEM((n // nx, 4 * blocks, members), BF16),
            pltpu.VMEM((blocks, obs, members), BF16),
            pltpu.VMEM((blocks, obs), BF16),
            pltpu.VMEM((blocks, obs), BF16),
            pltpu.VMEM((nx, patches, nlist), F32),
            pltpu.SMEM((nlist, lists.shape[1]), jnp.int32),
            pltpu.SMEM((1, lists.shape[1]), jnp.int32),
            pltpu.SMEM((nx, patches, nlist), F32),
            dma((patches * (-(-(n - 1) // BATCH)),)),
            dma((patches,)),
            dma((patches,)),
            dma((4,)),
            dma((4,)),
            dma((nz,)),
            dma((nz,)),
            dma((nz,)),
            dma((nz,)),
            dma((1,)),
            dma((1,)),
            dma((1,)),
            dma((1,)),
            dma((1,)),
            dma((7,)),
        ],
        compiler_params=pltpu.CompilerParams(
            collective_id=0, has_side_effects=True, vmem_limit_bytes=20 * 2**20
        ),
        name="analysis_kernel",
    )(
        *(
            pltpu.with_memory_space_constraint(operand, pltpu.HBM)
            for operand in (
                prior_states, anomalies[0], departure[0], precision[0], lists[0].T, tallies, localization[0]
            )
        )
    )


def solution(mesh):
    nx, nz = 4, mesh.shape["mem"] // 4
    return jax.shard_map(
        functools.partial(body, nx, nz, mesh.shape["cell"]),
        mesh=mesh,
        in_specs=(
            P("mem", "cell"),
            P("cell", "mem", None, None),
            P("cell", "mem", None),
            P("cell", "mem", None),
            P("cell", None, None),
            P("cell", None),
            P("cell", "mem", None),
        ),
        out_specs=P("mem", "cell"),
        check_vma=False,
    )
```

```python
import functools
import math

import jax
import jax.numpy as jnp
from jax import lax
from jax.experimental import pallas as pl
from jax.experimental.pallas import tpu as pltpu
from jax.sharding import PartitionSpec as P

ITERS = 4
WINDOW = 6
PACE = 4
BATCH = 8
CHUNK = 256
GROUP = 4

HIGHEST = lax.Precision.HIGHEST
MESH = pl.DeviceIdType.MESH
F32 = jnp.float32
BF16 = jnp.bfloat16


def iota(shape, axis):
    return lax.broadcasted_iota(jnp.int32, shape, axis)


def split(value):
    high = value.astype(BF16)
    return high, (value - high.astype(F32)).astype(BF16)


def fold(gram):
    half = gram.shape[0] // 2
    row, lane = iota((half, 2 * half), 0), iota((half, 2 * half), 1)
    return jnp.where(lane >= row, gram[:half], pltpu.roll(gram[half:], half, 1))


def unfold(folded, diagonal):
    half = folded.shape[0]
    row, lane = iota((2 * half, 2 * half), 0), iota((2 * half, 2 * half), 1)
    both = jnp.concatenate([folded, pltpu.roll(folded, half, 1)], axis=0)
    direct = ((row < half) & (lane >= row)) | ((row >= half) & (lane >= half) & (lane < row))
    full = jnp.where(direct, both, both.T)
    return jnp.where(row == lane, diagonal, full)


def with_tail(folded, diagonal, projected):
    parts = split(diagonal) + split(projected)
    rows = [part.astype(F32) for part in parts] + [jnp.zeros((4, folded.shape[1]), F32)]
    return jnp.concatenate([folded] + rows, axis=0).astype(BF16)


def from_tail(whole):
    half = whole.shape[0] - 8
    row = [whole[half + k : half + k + 1] for k in range(4)]
    return whole[:half], row[0] + row[1], row[2] + row[3]


def product(left, right):
    return jnp.dot(left, right, precision=HIGHEST, preferred_element_type=F32)


def transforms(grams, projections, ridge):
    size = grams[0].shape[0]
    identity = (iota((size, size), 0) == iota((size, size), 1)).astype(F32)
    systems = [ridge * identity + gram for gram in grams]
    levels = [jnp.sqrt(jnp.sum(system * system, keepdims=True)) for system in systems]
    approach = [system / level for system, level in zip(systems, levels)]
    inverse_root = [None] * len(grams)
    for sweep in range(ITERS):
        if sweep == 0:
            factor = [1.5 * identity - 0.5 * a for a in approach]
        else:
            factor = [1.5 * identity - 0.5 * product(r, a) for r, a in zip(inverse_root, approach)]
        if sweep < ITERS - 1:
            approach = [product(a, f) for a, f in zip(approach, factor)]
        inverse_root = factor if sweep == 0 else [product(f, r) for f, r in zip(factor, inverse_root)]
    result = []
    for inverse, level, projected in zip(inverse_root, levels, projections):
        root = inverse / jnp.sqrt(level)
        wide = jnp.broadcast_to(projected, (8, size))
        mean_shift = product(product(wide, root), root)[:1]
        result.append((math.sqrt(size - 1) * root + mean_shift).astype(BF16))
    return result


def kernel(
    nx, nz, ncell,
    x_ref, y_any, d_any, e_any, idx_any, tally_any, loc_any,
    out_ref,
    arrived, result, grams, sums_out, sums_in, sums_own, stats, partial, line_sums, cells, flat, change, dep, prec, lines, tails,
    y_ref, d_ref, e_ref, locs, idx_ref, tally_ref, loc_ref,
    in_send, in_recv, in_self, small_send, small_recv, z_send, z_recv, tail_send, tail_recv, x_send, x_recv,
    out_send, out_recv, out_self, load,
):
    n = nx * nz
    me, cell = lax.axis_index("mem"), lax.axis_index("cell")
    my_x, my_z = me // nz, me % nz
    patches, _, rows, points = arrived.shape
    blocks, obs, members = y_ref.shape
    half = members // 2
    nlist = loc_ref.shape[2]
    line = nz * blocks

    def peer(dx, dz):
        return lax.rem(my_x + dx + nx, nx) * nz + lax.rem(my_z + dz + nz, nz)

    def remote(src, dst, ssem, rsem, to):
        return pltpu.make_async_remote_copy(
            src_ref=src, dst_ref=dst, send_sem=ssem, recv_sem=rsem, device_id=to, device_id_type=MESH
        )

    def partner(o):
        turned = o + (cell % 2) * (n - 2 * o)
        return peer(turned // nz, turned % nz)

    barrier = pltpu.get_barrier_semaphore()

    for o in range(1, n):
        pl.semaphore_signal(barrier, inc=1, device_id={"mem": lax.rem(me + o, n)}, device_id_type=MESH)
    for o in range(1, ncell):
        pl.semaphore_signal(barrier, inc=1, device_id={"cell": lax.rem(cell + o, ncell)}, device_id_type=MESH)

    loads = [
        pltpu.make_async_copy(src, dst, load.at[k])
        for k, (src, dst) in enumerate(
            [(y_any, y_ref), (d_any, d_ref), (e_any, e_ref), (loc_any, locs.at[my_x]), (idx_any, idx_ref), (tally_any, tally_ref)]
        )
    ]
    for copy in loads:
        copy.start()

    pl.semaphore_wait(barrier, n - 1 + ncell - 1)

    def columns(owner, p):
        return pl.ds(pl.multiple_of((owner * patches + p) * points, 128), points)

    def own_in(p):
        return pltpu.make_async_copy(x_ref.at[:, columns(me, p)], arrived.at[p, me], in_self.at[p])

    batches = [(p, first) for p in range(patches) for first in range(1, n, BATCH)]
    sent, left = [], []

    def wait_in_send(k):
        p, first = batches[k]
        size = min(BATCH, n - first)
        ref = arrived.at[p, pl.ds(0, size)]
        remote(ref, ref, in_send.at[k], in_recv.at[p], {"mem": me}).wait_send()

    def pump(count=len(batches), window=WINDOW):
        for k in range(len(sent), min(len(sent) + count, len(batches))):
            p, first = batches[k]
            if k >= window:
                wait_in_send(k - window)
                left.append(k - window)
            if first == 1:
                own_in(p).start()

            @pl.loop(first, min(first + BATCH, n))
            def _(o):
                r = partner(o)
                remote(
                    x_ref.at[:, columns(r, p)], arrived.at[p, me], in_send.at[k], in_recv.at[p], {"mem": r}
                ).start()

            sent.append(k)

    pump(WINDOW)

    loads[3].wait()
    for dx in range(1, nx):
        ref = locs.at[my_x]
        remote(ref, ref, small_send.at[2], small_recv.at[2], {"mem": peer(dx, 0)}).start()
    for copy in loads[:3]:
        copy.wait()

    dep[...] = d_ref[...].astype(F32)
    prec[...] = e_ref[...].astype(F32)
    lane = iota((1, members), 1)
    diagonal_mask = iota((members, members), 0) == iota((members, members), 1)

    def one_block(b, tallied):
        y = y_ref[b]
        e, d = prec[pl.ds(b, 1), :], dep[pl.ds(b, 1), :]
        weighted = (y.astype(F32).T * e).astype(BF16)
        gram = jnp.dot(weighted, y, preferred_element_type=F32)
        high, low = split(e * d)
        row = iota((16, obs), 0)
        pair = jnp.where(row == 0, high.astype(F32), jnp.where(row == 1, low.astype(F32), 0.0)).astype(BF16)
        projected = jnp.sum(jnp.dot(pair, y, preferred_element_type=F32), axis=0, keepdims=True)
        diagonal = jnp.sum(jnp.where(diagonal_mask, gram, 0.0), axis=0, keepdims=True)
        grams[my_z * blocks + b] = fold(gram).astype(BF16)
        lines[pl.ds(b, 1), :] = diagonal
        lines[pl.ds(blocks + b, 1), :] = projected
        power = jnp.sum(e * d * d, keepdims=True)
        spread = jnp.sum(diagonal, keepdims=True)
        return tallied + jnp.where(lane == b, power, 0.0) + jnp.where(lane == blocks + b, spread, 0.0)

    stats[me] = lax.fori_loop(0, blocks, one_block, jnp.zeros((1, members), F32))
    pairs = split(lines[:blocks, :]) + split(lines[blocks:, :])
    tails[my_z] = jnp.concatenate([part.astype(F32) for part in pairs], axis=0).astype(BF16)

    def small_copy(which, buffer, place, to):
        return remote(buffer.at[place], buffer.at[place], small_send.at[which], small_recv.at[which], to)

    def wait_small(which, buffer, count):
        whole = buffer.at[pl.ds(0, count)]
        remote(whole, whole, small_send.at[which], small_recv.at[which], {"mem": me}).wait()

    for dz in range(1, nz):
        small_copy(3, stats, me, {"mem": peer(0, dz)}).start()

    first, second = (0, blocks // 2), (blocks // 2, blocks // 2)

    def along_z(shift, part, sem, step):
        start, size = part or (0, blocks)
        ref = grams.at[pl.ds(lax.rem(my_z + shift + nz, nz) * blocks + start, size)]
        return remote(ref, ref, z_send.at[sem], z_recv.at[sem], {"mem": peer(0, step)})

    def tail_along_z(shift, sem, step):
        ref = tails.at[lax.rem(my_z + shift + nz, nz)]
        return remote(ref, ref, tail_send.at[sem], tail_recv.at[sem], {"mem": peer(0, step)})

    reach = nz // 2

    def forward(step):
        last = step == reach - 1
        tail_along_z(-step, step, 1).start()
        if not last:
            tail_along_z(step, reach + step, -1).start()
        for block in range(blocks):
            if not last or block < blocks // 2:
                along_z(-step, (block, 1), step, 1).start()
            if not last or block >= blocks // 2:
                along_z(step, (block, 1), reach + step, -1).start()

    def receive(step):
        last = step == reach
        tail_along_z(-step, step - 1, 1).wait_recv()
        if not last:
            tail_along_z(step, reach + step - 1, -1).wait_recv()
        along_z(-step, first if last else None, step - 1, 1).wait_recv()
        along_z(step, second if last else None, reach + step - 1, -1).wait_recv()

    forward(0)
    loads[4].wait()
    loads[5].wait()
    wait_small(2, locs, nx - 1)
    to_scalar = pltpu.make_async_copy(locs, loc_ref, load.at[6])
    to_scalar.start()
    to_scalar.wait()

    def weight(x, p, s):
        active = jnp.clip(tally_ref[0, (x * nz + my_z) * patches + p] - s, 0, 1).astype(F32)
        return loc_ref[x, p, s] * active

    def listed(x, p, s):
        return idx_ref[s, (x * nz + my_z) * patches + p]

    pump(PACE)

    def add_request(p, total):
        for s in range(nlist):
            far = jnp.abs(block_at - listed(my_x, p, s))
            total = total + weight(my_x, p, s) * (1 - jnp.minimum(far, 1)).astype(F32)
        return total

    row, column = iota((n, members), 0), iota((n, members), 1)
    block_at = jnp.where(column < 2 * blocks, row * blocks + column % blocks, -1)
    asked = lax.fori_loop(0, patches, add_request, jnp.zeros((n, members), F32))
    my_line = pl.ds(my_x * nz, nz)
    wait_small(3, stats, nz - 1)
    for dx in range(1, nx):
        small_copy(4, stats, my_line, {"mem": peer(dx, 0)}).start()
    receive(1)
    forward(1)
    pump(PACE)

    wait_small(4, stats, (nx - 1) * nz)
    shares = asked * jnp.sum(stats[...], axis=1)
    partial[my_z] = jnp.sum(shares, axis=0, keepdims=True)
    for dz in range(1, nz):
        small_copy(0, partial, my_z, {"mem": peer(0, dz)}).start()
    receive(2)
    forward(2)
    pump(PACE)

    wait_small(0, partial, nz - 1)
    line_sums[my_x] = jnp.sum(partial[...], axis=0)
    for dx in range(1, nx):
        small_copy(5, line_sums, my_x, {"mem": peer(dx, 0)}).start()
    for step in range(3, reach):
        receive(step)
        forward(step)
        pump(PACE)

    wait_small(5, line_sums, nx - 1)
    cells[cell] = jnp.sum(line_sums[...], axis=0)

    @pl.loop(1, ncell)
    def _(o):
        small_copy(1, cells, cell, {"cell": lax.rem(cell + o, ncell)}).start()

    receive(reach)

    in_page = iota(tails.shape[1:], 0) % blocks

    def add_blocks(dx):
        x = lax.rem(my_x + dx, nx)

        @pl.loop(0, patches)
        def _(p):
            total, rest = jnp.zeros(grams.shape[1:], F32), jnp.zeros(tails.shape[1:], F32)
            for s in range(nlist):
                blk = listed(x, p, s)
                far = jnp.abs((blk >> (line.bit_length() - 1)) - my_x)
                w = weight(x, p, s) * (1 - jnp.minimum(far, 1)).astype(F32)
                place = blk & (line - 1)
                total = total + w * grams[place].astype(F32)
                hot = 1 - jnp.minimum(jnp.abs(in_page - (place & (blocks - 1))), 1)
                rest = rest + (w * hot.astype(F32)) * tails[place >> (blocks.bit_length() - 1)].astype(F32)
            diagonal = jnp.sum(rest[: 2 * blocks], axis=0, keepdims=True)
            projected = jnp.sum(rest[2 * blocks :], axis=0, keepdims=True)
            if dx:
                sums_out[dx - 1, p] = with_tail(total, diagonal, projected)
                remote(
                    sums_out.at[dx - 1, p], sums_in.at[dx - 1, p], x_send.at[0], x_recv.at[0], {"mem": peer(dx, 0)}
                ).start()
            else:
                none = jnp.zeros_like(diagonal)
                sums_own[p] = jnp.concatenate([total, diagonal, none, projected] + [none] * 5, axis=0)

    for dx in range(1, nx):
        add_blocks(dx)
    add_blocks(0)
    pump(PACE)
    remote(sums_in, sums_in, x_send.at[0], x_recv.at[0], {"mem": me}).wait()

    wait_small(1, cells, ncell - 1)
    sums = jnp.sum(cells[...], axis=0)
    power = jnp.sum(jnp.where(lane < blocks, sums, 0.0), keepdims=True)
    spread = jnp.sum(jnp.where((lane >= blocks) & (lane < 2 * blocks), sums, 0.0), keepdims=True) / (members - 1)
    ridge = (members - 1) / (power / spread)

    for step in range(reach):
        last = step == reach - 1
        tail_along_z(-step, step, 1).wait_send()
        if not last:
            tail_along_z(step, reach + step, -1).wait_send()
        along_z(-step, first if last else None, step, 1).wait_send()
        along_z(step, second if last else None, reach + step, -1).wait_send()

    pump(window=len(batches))

    def collect(p):
        total = sums_own[p]
        for k in range(nx - 1):
            total = total + sums_in[k, p].astype(F32)
        gram, diagonal, projected = from_tail(total)
        return unfold(gram, diagonal), projected

    @pl.loop(0, patches // GROUP)
    def _(g):
        pairs = [collect(g * GROUP + k) for k in range(GROUP)]
        made = transforms([a for a, _ in pairs], [b for _, b in pairs], ridge)
        for k in range(GROUP):
            change[g * GROUP + k] = made[k]

    @pl.loop(0, patches)
    def _(p):
        whole = arrived.at[p, pl.ds(0, n - 1)]
        remote(whole, whole, in_send.at[p], in_recv.at[p], {"mem": me}).wait_recv()
        own_in(p).wait()

        @pl.loop(0, points // CHUNK)
        def _(c):
            cut = pl.ds(pl.multiple_of(c * CHUNK, CHUNK), CHUNK)
            for m in range(n):
                flat[rows * m : rows * (m + 1), :] = arrived[p, m, :, cut].astype(F32)
            states = flat[...]
            means = jnp.sum(states, axis=0, keepdims=True) * (1.0 / members)
            deviation = (states - means).astype(BF16)
            updated = means + jnp.dot(change[p], deviation, preferred_element_type=F32)
            for m in range(n):
                result[p, m, :, cut] = updated[rows * m : rows * (m + 1), :].astype(BF16)

        pltpu.make_async_copy(result.at[p, me], out_ref.at[:, columns(me, p)], out_self.at[0]).start()
        @pl.loop(0, n)
        def _(q):
            r = lax.rem(my_x + q % nx, nx) * nz + (q // (2 * nx)) * 2 + lax.rem(my_z + (q // nx) % 2, 2)

            @pl.when(r != me)
            def _():
                remote(
                    result.at[p, r], out_ref.at[:, columns(me, p)], out_send.at[0], out_recv.at[0], {"mem": r}
                ).start()

    for k in range(len(left), len(batches)):
        wait_in_send(k)
    mine_out = pl.ds(pl.multiple_of(me * patches * points, 128), patches * points)
    pltpu.make_async_copy(out_ref.at[:, mine_out], out_ref.at[:, mine_out], out_self.at[0]).wait()
    others = out_ref.at[:, pl.ds(0, (n - 1) * patches * points)]
    remote(others, others, out_send.at[0], out_recv.at[0], {"mem": me}).wait()


def body(nx, nz, ncell, prior_states, anomalies, departure, precision, lists, tallies, localization):
    n = nx * nz
    rows, cells = prior_states.shape
    patches, nlist = localization.shape[1:]
    points = cells // (n * patches)
    blocks, obs, members = anomalies.shape[1:]
    anywhere = pl.BlockSpec(memory_space=pl.ANY)
    dma = pltpu.SemaphoreType.DMA
    return pl.pallas_call(
        functools.partial(kernel, nx, nz, ncell),
        out_shape=pltpu.VMEM((rows, cells), BF16),
        in_specs=[anywhere] * 7,
        out_specs=anywhere,
        scratch_shapes=[
            pltpu.VMEM((patches, n, rows, points), BF16),
            pltpu.VMEM((patches, n, rows, points), BF16),
            pltpu.VMEM((n // nx * blocks, members // 2, members), BF16),
            pltpu.VMEM((nx - 1, patches, members // 2 + 8, members), BF16),
            pltpu.VMEM((nx - 1, patches, members // 2 + 8, members), BF16),
            pltpu.VMEM((patches, members // 2 + 8, members), F32),
            pltpu.VMEM((n, 1, members), F32),
            pltpu.VMEM((n // nx, 1, members), F32),
            pltpu.VMEM((nx, 1, members), F32),
            pltpu.VMEM((ncell, 1, members), F32),
            pltpu.VMEM((members, CHUNK), F32),
            pltpu.VMEM((patches, members, members), BF16),
            pltpu.VMEM((blocks, obs), F32),
            pltpu.VMEM((blocks, obs), F32),
            pltpu.VMEM((2 * blocks, members), F32),
            pltpu.VMEM((n // nx, 4 * blocks, members), BF16),
            pltpu.VMEM((blocks, obs, members), BF16),
            pltpu.VMEM((blocks, obs), BF16),
            pltpu.VMEM((blocks, obs), BF16),
            pltpu.VMEM((nx, patches, nlist), F32),
            pltpu.SMEM((nlist, lists.shape[1]), jnp.int32),
            pltpu.SMEM((1, lists.shape[1]), jnp.int32),
            pltpu.SMEM((nx, patches, nlist), F32),
            dma((patches * (-(-(n - 1) // BATCH)),)),
            dma((patches,)),
            dma((patches,)),
            dma((6,)),
            dma((6,)),
            dma((nz,)),
            dma((nz,)),
            dma((nz,)),
            dma((nz,)),
            dma((1,)),
            dma((1,)),
            dma((1,)),
            dma((1,)),
            dma((1,)),
            dma((7,)),
        ],
        compiler_params=pltpu.CompilerParams(
            collective_id=0, has_side_effects=True, vmem_limit_bytes=20 * 2**20
        ),
        name="analysis_kernel",
    )(
        *(
            pltpu.with_memory_space_constraint(operand, pltpu.HBM)
            for operand in (
                prior_states, anomalies[0], departure[0], precision[0], lists[0].T, tallies, localization[0]
            )
        )
    )


def solution(mesh):
    nx, nz = 4, mesh.shape["mem"] // 4
    return jax.shard_map(
        functools.partial(body, nx, nz, mesh.shape["cell"]),
        mesh=mesh,
        in_specs=(
            P("mem", "cell"),
            P("cell", "mem", None, None),
            P("cell", "mem", None),
            P("cell", "mem", None),
            P("cell", None, None),
            P("cell", None),
            P("cell", "mem", None),
        ),
        out_specs=P("mem", "cell"),
        check_vma=False,
    )
```

```python
import functools
import math

import jax
import jax.numpy as jnp
from jax import lax
from jax.experimental import pallas as pl
from jax.experimental.pallas import tpu as pltpu
from jax.sharding import PartitionSpec as P

ITERS = 4
WINDOW = 6
PACE = 4
BATCH = 8
CHUNK = 256
GROUP = 4

HIGHEST = lax.Precision.HIGHEST
MESH = pl.DeviceIdType.MESH
F32 = jnp.float32
BF16 = jnp.bfloat16


def iota(shape, axis):
    return lax.broadcasted_iota(jnp.int32, shape, axis)


def split(value):
    high = value.astype(BF16)
    return high, (value - high.astype(F32)).astype(BF16)


def fold(gram):
    half = gram.shape[0] // 2
    row, lane = iota((half, 2 * half), 0), iota((half, 2 * half), 1)
    return jnp.where(lane >= row, gram[:half], pltpu.roll(gram[half:], half, 1))


def unfold(folded, diagonal):
    half = folded.shape[0]
    row, lane = iota((2 * half, 2 * half), 0), iota((2 * half, 2 * half), 1)
    both = jnp.concatenate([folded, pltpu.roll(folded, half, 1)], axis=0)
    direct = ((row < half) & (lane >= row)) | ((row >= half) & (lane >= half) & (lane < row))
    full = jnp.where(direct, both, both.T)
    return jnp.where(row == lane, diagonal, full)


def with_tail(folded, diagonal, projected):
    parts = split(diagonal) + split(projected)
    rows = [part.astype(F32) for part in parts] + [jnp.zeros((4, folded.shape[1]), F32)]
    return jnp.concatenate([folded] + rows, axis=0).astype(BF16)


def from_tail(whole):
    half = whole.shape[0] - 8
    row = [whole[half + k : half + k + 1] for k in range(4)]
    return whole[:half], row[0] + row[1], row[2] + row[3]


def product(left, right):
    return jnp.dot(left, right, precision=HIGHEST, preferred_element_type=F32)


def transforms(grams, projections, ridge):
    size = grams[0].shape[0]
    identity = (iota((size, size), 0) == iota((size, size), 1)).astype(F32)
    systems = [ridge * identity + gram for gram in grams]
    levels = [jnp.sqrt(jnp.sum(system * system, keepdims=True)) for system in systems]
    approach = [system / level for system, level in zip(systems, levels)]
    inverse_root = [None] * len(grams)
    for sweep in range(ITERS):
        if sweep == 0:
            factor = [1.5 * identity - 0.5 * a for a in approach]
        else:
            factor = [1.5 * identity - 0.5 * product(r, a) for r, a in zip(inverse_root, approach)]
        if sweep < ITERS - 1:
            approach = [product(a, f) for a, f in zip(approach, factor)]
        inverse_root = factor if sweep == 0 else [product(f, r) for f, r in zip(factor, inverse_root)]
    result = []
    for inverse, level, projected in zip(inverse_root, levels, projections):
        root = inverse / jnp.sqrt(level)
        wide = jnp.broadcast_to(projected, (8, size))
        mean_shift = product(product(wide, root), root)[:1]
        result.append((math.sqrt(size - 1) * root + mean_shift).astype(BF16))
    return result


def kernel(
    nx, nz, ncell,
    x_ref, y_any, d_any, e_any, idx_any, tally_any, loc_any,
    out_ref,
    arrived, result, grams, sums_out, sums_in, sums_own, stats, partial, line_sums, cells, flat, change, dep, prec, lines, tails,
    y_ref, d_ref, e_ref, locs, idx_ref, tally_ref, loc_ref,
    in_send, in_recv, in_self, small_send, small_recv, z_send, z_recv, tail_send, tail_recv, x_send, x_recv,
    out_send, out_recv, out_self, load, states_ref,
):
    n = nx * nz
    me, cell = lax.axis_index("mem"), lax.axis_index("cell")
    my_x, my_z = me // nz, me % nz
    patches, _, rows, points = arrived.shape
    blocks, obs, members = y_ref.shape
    half = members // 2
    nlist = loc_ref.shape[2]
    line = nz * blocks

    def peer(dx, dz):
        return lax.rem(my_x + dx + nx, nx) * nz + lax.rem(my_z + dz + nz, nz)

    def remote(src, dst, ssem, rsem, to):
        return pltpu.make_async_remote_copy(
            src_ref=src, dst_ref=dst, send_sem=ssem, recv_sem=rsem, device_id=to, device_id_type=MESH
        )

    def partner(o):
        turned = o + (cell % 2) * (n - 2 * o)
        return peer(turned // nz, turned % nz)

    barrier = pltpu.get_barrier_semaphore()

    for o in range(1, n):
        pl.semaphore_signal(barrier, inc=1, device_id={"mem": lax.rem(me + o, n)}, device_id_type=MESH)
    for o in range(1, ncell):
        pl.semaphore_signal(barrier, inc=1, device_id={"cell": lax.rem(cell + o, ncell)}, device_id_type=MESH)

    whole_states = pltpu.make_async_copy(x_ref, states_ref, load.at[7])
    whole_states.start()
    loads = [
        pltpu.make_async_copy(src, dst, load.at[k])
        for k, (src, dst) in enumerate(
            [(y_any, y_ref), (d_any, d_ref), (e_any, e_ref), (loc_any, locs.at[my_x]), (idx_any, idx_ref), (tally_any, tally_ref)]
        )
    ]
    for copy in loads:
        copy.start()

    pl.semaphore_wait(barrier, n - 1 + ncell - 1)
    whole_states.wait()

    def columns(owner, p):
        return pl.ds(pl.multiple_of((owner * patches + p) * points, 128), points)

    def own_in(p):
        return pltpu.make_async_copy(states_ref.at[:, columns(me, p)], arrived.at[p, me], in_self.at[p])

    batches = [(p, first) for p in range(patches) for first in range(1, n, BATCH)]
    sent, left = [], []

    def wait_in_send(k):
        p, first = batches[k]
        size = min(BATCH, n - first)
        ref = arrived.at[p, pl.ds(0, size)]
        remote(ref, ref, in_send.at[k], in_recv.at[p], {"mem": me}).wait_send()

    def pump(count=len(batches), window=WINDOW):
        for k in range(len(sent), min(len(sent) + count, len(batches))):
            p, first = batches[k]
            if k >= window:
                wait_in_send(k - window)
                left.append(k - window)
            if first == 1:
                own_in(p).start()

            @pl.loop(first, min(first + BATCH, n))
            def _(o):
                r = partner(o)
                remote(
                    states_ref.at[:, columns(r, p)], arrived.at[p, me], in_send.at[k], in_recv.at[p], {"mem": r}
                ).start()

            sent.append(k)

    pump(WINDOW)

    loads[3].wait()
    for dx in range(1, nx):
        ref = locs.at[my_x]
        remote(ref, ref, small_send.at[2], small_recv.at[2], {"mem": peer(dx, 0)}).start()
    for copy in loads[:3]:
        copy.wait()

    dep[...] = d_ref[...].astype(F32)
    prec[...] = e_ref[...].astype(F32)
    lane = iota((1, members), 1)
    diagonal_mask = iota((members, members), 0) == iota((members, members), 1)

    def one_block(b, tallied):
        y = y_ref[b]
        e, d = prec[pl.ds(b, 1), :], dep[pl.ds(b, 1), :]
        weighted = (y.astype(F32).T * e).astype(BF16)
        gram = jnp.dot(weighted, y, preferred_element_type=F32)
        high, low = split(e * d)
        row = iota((16, obs), 0)
        pair = jnp.where(row == 0, high.astype(F32), jnp.where(row == 1, low.astype(F32), 0.0)).astype(BF16)
        projected = jnp.sum(jnp.dot(pair, y, preferred_element_type=F32), axis=0, keepdims=True)
        diagonal = jnp.sum(jnp.where(diagonal_mask, gram, 0.0), axis=0, keepdims=True)
        grams[my_z * blocks + b] = fold(gram).astype(BF16)
        lines[pl.ds(b, 1), :] = diagonal
        lines[pl.ds(blocks + b, 1), :] = projected
        power = jnp.sum(e * d * d, keepdims=True)
        spread = jnp.sum(diagonal, keepdims=True)
        return tallied + jnp.where(lane == b, power, 0.0) + jnp.where(lane == blocks + b, spread, 0.0)

    stats[me] = lax.fori_loop(0, blocks, one_block, jnp.zeros((1, members), F32))
    pairs = split(lines[:blocks, :]) + split(lines[blocks:, :])
    tails[my_z] = jnp.concatenate([part.astype(F32) for part in pairs], axis=0).astype(BF16)

    def small_copy(which, buffer, place, to):
        return remote(buffer.at[place], buffer.at[place], small_send.at[which], small_recv.at[which], to)

    def wait_small(which, buffer, count):
        whole = buffer.at[pl.ds(0, count)]
        remote(whole, whole, small_send.at[which], small_recv.at[which], {"mem": me}).wait()

    for dz in range(1, nz):
        small_copy(3, stats, me, {"mem": peer(0, dz)}).start()

    first, second = (0, blocks // 2), (blocks // 2, blocks // 2)

    def along_z(shift, part, sem, step):
        start, size = part or (0, blocks)
        ref = grams.at[pl.ds(lax.rem(my_z + shift + nz, nz) * blocks + start, size)]
        return remote(ref, ref, z_send.at[sem], z_recv.at[sem], {"mem": peer(0, step)})

    def tail_along_z(shift, sem, step):
        ref = tails.at[lax.rem(my_z + shift + nz, nz)]
        return remote(ref, ref, tail_send.at[sem], tail_recv.at[sem], {"mem": peer(0, step)})

    reach = nz // 2

    def forward(step):
        last = step == reach - 1
        tail_along_z(-step, step, 1).start()
        if not last:
            tail_along_z(step, reach + step, -1).start()
        for block in range(blocks):
            if not last or block < blocks // 2:
                along_z(-step, (block, 1), step, 1).start()
            if not last or block >= blocks // 2:
                along_z(step, (block, 1), reach + step, -1).start()

    def receive(step):
        last = step == reach
        tail_along_z(-step, step - 1, 1).wait_recv()
        if not last:
            tail_along_z(step, reach + step - 1, -1).wait_recv()
        along_z(-step, first if last else None, step - 1, 1).wait_recv()
        along_z(step, second if last else None, reach + step - 1, -1).wait_recv()

    forward(0)
    loads[4].wait()
    loads[5].wait()
    wait_small(2, locs, nx - 1)
    to_scalar = pltpu.make_async_copy(locs, loc_ref, load.at[6])
    to_scalar.start()
    to_scalar.wait()

    def weight(x, p, s):
        active = jnp.clip(tally_ref[0, (x * nz + my_z) * patches + p] - s, 0, 1).astype(F32)
        return loc_ref[x, p, s] * active

    def listed(x, p, s):
        return idx_ref[s, (x * nz + my_z) * patches + p]

    pump(PACE)

    def add_request(p, total):
        for s in range(nlist):
            far = jnp.abs(block_at - listed(my_x, p, s))
            total = total + weight(my_x, p, s) * (1 - jnp.minimum(far, 1)).astype(F32)
        return total

    row, column = iota((n, members), 0), iota((n, members), 1)
    block_at = jnp.where(column < 2 * blocks, row * blocks + column % blocks, -1)
    asked = lax.fori_loop(0, patches, add_request, jnp.zeros((n, members), F32))
    my_line = pl.ds(my_x * nz, nz)
    wait_small(3, stats, nz - 1)
    for dx in range(1, nx):
        small_copy(4, stats, my_line, {"mem": peer(dx, 0)}).start()
    receive(1)
    forward(1)
    pump(PACE)

    wait_small(4, stats, (nx - 1) * nz)
    shares = asked * jnp.sum(stats[...], axis=1)
    partial[my_z] = jnp.sum(shares, axis=0, keepdims=True)
    for dz in range(1, nz):
        small_copy(0, partial, my_z, {"mem": peer(0, dz)}).start()
    receive(2)
    forward(2)
    pump(PACE)

    wait_small(0, partial, nz - 1)
    line_sums[my_x] = jnp.sum(partial[...], axis=0)
    for dx in range(1, nx):
        small_copy(5, line_sums, my_x, {"mem": peer(dx, 0)}).start()
    for step in range(3, reach):
        receive(step)
        forward(step)
        pump(PACE)

    wait_small(5, line_sums, nx - 1)
    cells[cell] = jnp.sum(line_sums[...], axis=0)

    @pl.loop(1, ncell)
    def _(o):
        small_copy(1, cells, cell, {"cell": lax.rem(cell + o, ncell)}).start()

    receive(reach)

    in_page = iota(tails.shape[1:], 0) % blocks

    def add_blocks(dx):
        x = lax.rem(my_x + dx, nx)

        @pl.loop(0, patches)
        def _(p):
            total, rest = jnp.zeros(grams.shape[1:], F32), jnp.zeros(tails.shape[1:], F32)
            for s in range(nlist):
                blk = listed(x, p, s)
                far = jnp.abs((blk >> (line.bit_length() - 1)) - my_x)
                w = weight(x, p, s) * (1 - jnp.minimum(far, 1)).astype(F32)
                place = blk & (line - 1)
                total = total + w * grams[place].astype(F32)
                hot = 1 - jnp.minimum(jnp.abs(in_page - (place & (blocks - 1))), 1)
                rest = rest + (w * hot.astype(F32)) * tails[place >> (blocks.bit_length() - 1)].astype(F32)
            diagonal = jnp.sum(rest[: 2 * blocks], axis=0, keepdims=True)
            projected = jnp.sum(rest[2 * blocks :], axis=0, keepdims=True)
            if dx:
                sums_out[dx - 1, p] = with_tail(total, diagonal, projected)
                remote(
                    sums_out.at[dx - 1, p], sums_in.at[dx - 1, p], x_send.at[0], x_recv.at[0], {"mem": peer(dx, 0)}
                ).start()
            else:
                none = jnp.zeros_like(diagonal)
                sums_own[p] = jnp.concatenate([total, diagonal, none, projected] + [none] * 5, axis=0)

    for dx in range(1, nx):
        add_blocks(dx)
    add_blocks(0)
    pump(PACE)
    remote(sums_in, sums_in, x_send.at[0], x_recv.at[0], {"mem": me}).wait()

    wait_small(1, cells, ncell - 1)
    sums = jnp.sum(cells[...], axis=0)
    power = jnp.sum(jnp.where(lane < blocks, sums, 0.0), keepdims=True)
    spread = jnp.sum(jnp.where((lane >= blocks) & (lane < 2 * blocks), sums, 0.0), keepdims=True) / (members - 1)
    ridge = (members - 1) / (power / spread)

    for step in range(reach):
        last = step == reach - 1
        tail_along_z(-step, step, 1).wait_send()
        if not last:
            tail_along_z(step, reach + step, -1).wait_send()
        along_z(-step, first if last else None, step, 1).wait_send()
        along_z(step, second if last else None, reach + step, -1).wait_send()

    pump(window=len(batches))

    def collect(p):
        total = sums_own[p]
        for k in range(nx - 1):
            total = total + sums_in[k, p].astype(F32)
        gram, diagonal, projected = from_tail(total)
        return unfold(gram, diagonal), projected

    @pl.loop(0, patches // GROUP)
    def _(g):
        pairs = [collect(g * GROUP + k) for k in range(GROUP)]
        made = transforms([a for a, _ in pairs], [b for _, b in pairs], ridge)
        for k in range(GROUP):
            change[g * GROUP + k] = made[k]

    @pl.loop(0, patches)
    def _(p):
        whole = arrived.at[p, pl.ds(0, n - 1)]
        remote(whole, whole, in_send.at[p], in_recv.at[p], {"mem": me}).wait_recv()
        own_in(p).wait()

        @pl.loop(0, points // CHUNK)
        def _(c):
            cut = pl.ds(pl.multiple_of(c * CHUNK, CHUNK), CHUNK)
            for m in range(n):
                flat[rows * m : rows * (m + 1), :] = arrived[p, m, :, cut].astype(F32)
            states = flat[...]
            means = jnp.sum(states, axis=0, keepdims=True) * (1.0 / members)
            deviation = (states - means).astype(BF16)
            updated = means + jnp.dot(change[p], deviation, preferred_element_type=F32)
            for m in range(n):
                result[p, m, :, cut] = updated[rows * m : rows * (m + 1), :].astype(BF16)

        pltpu.make_async_copy(result.at[p, me], out_ref.at[:, columns(me, p)], out_self.at[0]).start()
        @pl.loop(0, n)
        def _(q):
            r = lax.rem(my_x + q % nx, nx) * nz + (q // (2 * nx)) * 2 + lax.rem(my_z + (q // nx) % 2, 2)

            @pl.when(r != me)
            def _():
                remote(
                    result.at[p, r], out_ref.at[:, columns(me, p)], out_send.at[0], out_recv.at[0], {"mem": r}
                ).start()

    for k in range(len(left), len(batches)):
        wait_in_send(k)
    mine_out = pl.ds(pl.multiple_of(me * patches * points, 128), patches * points)
    pltpu.make_async_copy(out_ref.at[:, mine_out], out_ref.at[:, mine_out], out_self.at[0]).wait()
    others = out_ref.at[:, pl.ds(0, (n - 1) * patches * points)]
    remote(others, others, out_send.at[0], out_recv.at[0], {"mem": me}).wait()


def body(nx, nz, ncell, prior_states, anomalies, departure, precision, lists, tallies, localization):
    n = nx * nz
    rows, cells = prior_states.shape
    patches, nlist = localization.shape[1:]
    points = cells // (n * patches)
    blocks, obs, members = anomalies.shape[1:]
    anywhere = pl.BlockSpec(memory_space=pl.ANY)
    dma = pltpu.SemaphoreType.DMA
    return pl.pallas_call(
        functools.partial(kernel, nx, nz, ncell),
        out_shape=pltpu.VMEM((rows, cells), BF16),
        in_specs=[anywhere] * 7,
        out_specs=anywhere,
        scratch_shapes=[
            pltpu.VMEM((patches, n, rows, points), BF16),
            pltpu.VMEM((patches, n, rows, points), BF16),
            pltpu.VMEM((n // nx * blocks, members // 2, members), BF16),
            pltpu.VMEM((nx - 1, patches, members // 2 + 8, members), BF16),
            pltpu.VMEM((nx - 1, patches, members // 2 + 8, members), BF16),
            pltpu.VMEM((patches, members // 2 + 8, members), F32),
            pltpu.VMEM((n, 1, members), F32),
            pltpu.VMEM((n // nx, 1, members), F32),
            pltpu.VMEM((nx, 1, members), F32),
            pltpu.VMEM((ncell, 1, members), F32),
            pltpu.VMEM((members, CHUNK), F32),
            pltpu.VMEM((patches, members, members), BF16),
            pltpu.VMEM((blocks, obs), F32),
            pltpu.VMEM((blocks, obs), F32),
            pltpu.VMEM((2 * blocks, members), F32),
            pltpu.VMEM((n // nx, 4 * blocks, members), BF16),
            pltpu.VMEM((blocks, obs, members), BF16),
            pltpu.VMEM((blocks, obs), BF16),
            pltpu.VMEM((blocks, obs), BF16),
            pltpu.VMEM((nx, patches, nlist), F32),
            pltpu.SMEM((nlist, lists.shape[1]), jnp.int32),
            pltpu.SMEM((1, lists.shape[1]), jnp.int32),
            pltpu.SMEM((nx, patches, nlist), F32),
            dma((patches * (-(-(n - 1) // BATCH)),)),
            dma((patches,)),
            dma((patches,)),
            dma((6,)),
            dma((6,)),
            dma((nz,)),
            dma((nz,)),
            dma((nz,)),
            dma((nz,)),
            dma((1,)),
            dma((1,)),
            dma((1,)),
            dma((1,)),
            dma((1,)),
            dma((8,)),
            pltpu.VMEM((rows, cells), BF16),
        ],
        compiler_params=pltpu.CompilerParams(
            collective_id=0, has_side_effects=True, vmem_limit_bytes=20 * 2**20
        ),
        name="analysis_kernel",
    )(
        *(
            pltpu.with_memory_space_constraint(operand, pltpu.HBM)
            for operand in (
                prior_states, anomalies[0], departure[0], precision[0], lists[0].T, tallies, localization[0]
            )
        )
    )


def solution(mesh):
    nx, nz = 4, mesh.shape["mem"] // 4
    return jax.shard_map(
        functools.partial(body, nx, nz, mesh.shape["cell"]),
        mesh=mesh,
        in_specs=(
            P("mem", "cell"),
            P("cell", "mem", None, None),
            P("cell", "mem", None),
            P("cell", "mem", None),
            P("cell", None, None),
            P("cell", None),
            P("cell", "mem", None),
        ),
        out_specs=P("mem", "cell"),
        check_vma=False,
    )
```
